128 devices in a mesh: row: 8 (over y, x_lo), col: 16 (over x_hi, z, core).
Axes of the slice: x: 4 (x_hi: 2, x_lo: 2; x = x_hi * 2 + x_lo), y: 4, z: 4, core: 2. Of those that a mesh axis runs over, the one named last changes fastest.
Arguments:
- centres: float32 [40960, 64], P(('row', 'col')), may hold values from -6 to 6
- targets: float32 [40960, 16], P(('row', 'col')), may hold values from -6 to 6
- start_weights: float32 [40960, 16], P(('row', 'col')), may hold values from -6 to 6
Outputs:
- weighted: float32 [40960, 16], P(('row', 'col'))
- residual: float32 [40960, 16], P(('row', 'col'))
The draws below stay inside these ranges and needn't reach their ends.
All inputs are finite; a program needn't handle non-finite values.
Results may differ from the reference program's by a relative error of at most 0.0003.
Values sent between devices are 32-bit elements; how exact they have to be, the bound alone decides.
No kernel may reach another device: no remote copies, remote signals or barrier semaphores. Data moves between devices by JAX's collectives and lax.ppermute only.
A program may use at most 128 MiB of HBM per device.

```python
import math
import jax
import jax.numpy as jnp
from jax import lax

F = 64
TGT = 16
BLK = 320
ITERS = 2
NCEN = 40960


def draw_centres(key, part):
    key = jax.random.fold_in(key, 11)
    key_label, key_place, key_value = jax.random.split(key, 3)
    spread = 0.75
    labels = jax.random.randint(key_label, (NCEN // BLK,), 0, 4)
    member = jnp.repeat(labels, BLK)
    places = jax.random.normal(key_place, (4, F), jnp.float32) * 1.5
    values = jax.random.normal(key_value, (NCEN, F), jnp.float32)
    return jnp.clip((values + places[member]) * spread, -6.0, 6.0)


def draw_start_weights(key, part):
    key = jax.random.fold_in(key, 23)
    key_sign, key_level, key_noise = jax.random.split(key, 3)
    signs = jnp.where(jax.random.randint(key_sign, (1, TGT), 0, 2) == 0, -1.0, 1.0).astype(jnp.float32)
    level = jax.random.uniform(key_level, (1, TGT), jnp.float32, 0.6, 1.6)
    noise = jnp.clip(jax.random.normal(key_noise, (NCEN, TGT), jnp.float32) * 0.6, -3.0, 3.0)
    return jnp.clip(signs * level + noise, -6.0, 6.0)


def steps_of(own_key, shape, cuts, smallest, top_value):
    level, own = 1.0, jax.random.fold_in(own_key, 6)
    for axis_at, blocks in cuts:
        steps = jnp.exp(jax.random.uniform(jax.random.fold_in(own, axis_at), (blocks,), jnp.float32, smallest / len(cuts), top_value / len(cuts)))
        level = level * jnp.repeat(steps, shape[axis_at] // blocks).reshape([-1 if axis == axis_at else 1 for axis in range(len(shape))])
    return level


def gaussian(stream_key, shape, scale, reach, cuts=(), kind=jnp.bfloat16):
    entries = scale * jax.random.normal(stream_key, shape, jnp.float32)
    if cuts:
        entries = entries * steps_of(stream_key, shape, cuts, -0.22, 0.18)
    return jnp.clip(entries, -reach, reach).astype(kind)


def setup_inputs(seed: int = 0) -> dict:
    key_of = jax.random.split(jax.random.key(seed), 4)
    centres = draw_centres(jax.random.fold_in(key_of[3], 71), 0)
    targets = gaussian(key_of[1], (NCEN, TGT), 1.0, 6.0, ((0, 128),), jnp.float32)
    start_weights = draw_start_weights(jax.random.fold_in(key_of[3], 71), 0)
    return dict(centres=centres, targets=targets, start_weights=start_weights)


kernel_width = 2.0
soften = 0.01
ridge_term = 0.25

def kernel_block(left_pts, right_pts):
    left_sq = lax.optimization_barrier(jnp.sum(left_pts * left_pts, axis=1))[:, None]
    right_sq = lax.optimization_barrier(jnp.sum(right_pts * right_pts, axis=1))[None, :]
    cross = jnp.dot(left_pts, right_pts.T, precision=lax.Precision.HIGHEST, preferred_element_type=jnp.float32)
    return jnp.exp(-jnp.sqrt(left_sq + right_sq - 2.0 * cross + soften) / kernel_width)

def reference(centres, targets, start_weights):
    nrows = centres.shape[0]
    height = math.gcd(nrows, 1024)
    stacked = centres.reshape(nrows // height, height, centres.shape[1])
    totals = lax.map(lambda left_pts: lax.optimization_barrier(jnp.sum(kernel_block(left_pts, centres), axis=1)), stacked).reshape(nrows)
    weighted = start_weights
    residual = targets
    for step in range(ITERS):
        scaled = weighted / totals[:, None]
        applied = lax.map(lambda left_pts: jnp.dot(kernel_block(left_pts, centres), scaled, precision=lax.Precision.HIGHEST, preferred_element_type=jnp.float32), stacked).reshape(nrows, scaled.shape[1])
        residual = targets - applied - ridge_term * weighted
        weighted = weighted + residual
    return (weighted, residual)
```

```python
import jax
import jax.numpy as jnp
from jax import lax
from jax.experimental import pallas as pl
from jax.experimental.pallas import tpu as pltpu
from jax.sharding import Mesh, PartitionSpec as P

ITERS = 2

kernel_width = 2.0
soften = 0.01
ridge_term = 0.25

SCALE = 1.4426950408889634 / kernel_width
FLOOR = soften * SCALE * SCALE

f32 = jnp.float32
bf16 = jnp.bfloat16

AXES = ("y", "xl", "xh", "z", "k")
BLK = 320
FEAT = 64
TGT = 16
QUART = 4 * BLK
COLS = 8 * BLK
HALF = COLS // 2
IN_VMEM = 2

WHOLE = pl.BlockSpec(memory_space=pltpu.VMEM)
ANY = pl.BlockSpec(memory_space=pl.ANY)


def params(mib):
    return pltpu.CompilerParams(vmem_limit_bytes=mib << 20)


def parts_of(pts):
    scaled = pts * SCALE
    high = scaled.astype(bf16)
    low = (scaled - high.astype(f32)).astype(bf16)
    kept = high.astype(f32) + low.astype(f32)
    return high, low, jnp.sum(kept * kept, axis=0, keepdims=True)


def gram_setup(rows_ref, cols_ref, lhs, rhs, row_sq, col_sq):
    high, low, sq = parts_of(cols_ref[0:FEAT, :])
    rhs[0:64, :] = high
    rhs[64:128, :] = low
    rhs[128:192, :] = high
    rhs[192:256, :] = low
    col_sq[...] = sq
    pts = rows_ref[0:FEAT, :].T * SCALE
    high = pts.astype(bf16)
    low = (pts - high.astype(f32)).astype(bf16)
    kept = high.astype(f32) + low.astype(f32)
    row_sq[...] = jnp.sum(kept * kept, axis=1, keepdims=True) + FLOOR
    lhs[...] = jnp.concatenate([high, high, low, low], axis=1) * jnp.asarray(2.0, bf16)


def gram_cols(lhs, rhs_part, row_sq, col_part):
    cross = jnp.dot(lhs[...], rhs_part, preferred_element_type=f32)
    dist = jnp.maximum((row_sq[...] - cross) + col_part, FLOOR)
    return jnp.exp2(-(dist * lax.rsqrt(dist)))


def fold_lanes(part):
    acc = part[:, 0:128]
    for at in range(128, part.shape[1], 128):
        acc = acc + part[:, at : at + 128]
    return acc


def put_totals(acc, tot_ref):
    line = jnp.sum(acc.T, axis=0, keepdims=True)
    for m in range(4):
        tot_ref[m : m + 1, :] = line[:, m * BLK : (m + 1) * BLK]


def gram_quarter(rows, cols, keep):
    scratch = [
        pltpu.VMEM((QUART, 256), bf16),
        pltpu.VMEM((256, COLS), bf16),
        pltpu.VMEM((QUART, 1), f32),
        pltpu.VMEM((1, COLS), f32),
        pltpu.VMEM((QUART, 128), f32),
    ]
    step_cols = 256 if keep else 512

    def kept_body(rows_ref, cols_ref, out_ref, tot_ref, lhs, rhs, row_sq, col_sq, acc):
        gram_setup(rows_ref, cols_ref, lhs, rhs, row_sq, col_sq)
        for at in range(0, COLS, step_cols):
            part = gram_cols(lhs, rhs[:, at : at + step_cols], row_sq, col_sq[:, at : at + step_cols])
            out_ref[:, at : at + step_cols] = part
            if at:
                acc[...] += fold_lanes(part)
            else:
                acc[...] = fold_lanes(part)
        put_totals(acc[...], tot_ref)

    def sent_body(rows_ref, cols_ref, out_ref, tot_ref, lhs, rhs, row_sq, col_sq, acc):
        step = pl.program_id(0)

        @pl.when(step == 0)
        def _():
            gram_setup(rows_ref, cols_ref, lhs, rhs, row_sq, col_sq)
            acc[...] = jnp.zeros_like(acc)

        here = pl.ds(pl.multiple_of(step * step_cols, step_cols), step_cols)
        part = gram_cols(lhs, rhs[:, here], row_sq, col_sq[:, here])
        out_ref[...] = part
        acc[...] += fold_lanes(part)

        @pl.when(step == pl.num_programs(0) - 1)
        def _():
            put_totals(acc[...], tot_ref)

    tot = jax.ShapeDtypeStruct((4, BLK), f32)
    if keep:
        return pl.pallas_call(
            kept_body,
            in_specs=[WHOLE, WHOLE],
            out_specs=[WHOLE, WHOLE],
            out_shape=[pltpu.VMEM((QUART, COLS), f32), tot],
            scratch_shapes=scratch,
            compiler_params=params(20),
            name="gram_kept",
        )(rows, cols)
    return pl.pallas_call(
        sent_body,
        grid=(COLS // step_cols,),
        in_specs=[pl.BlockSpec(rows.shape, lambda j: (0, 0)), pl.BlockSpec(cols.shape, lambda j: (0, 0))],
        out_specs=[pl.BlockSpec((QUART, step_cols), lambda j: (0, j)), pl.BlockSpec((4, BLK), lambda j: (0, 0))],
        out_shape=[jax.ShapeDtypeStruct((QUART, COLS), f32), tot],
        scratch_shapes=scratch,
        compiler_params=params(24),
        name="gram_sent",
    )(rows, cols)


def two_terms(vals):
    high = vals.astype(bf16)
    return high, (vals - high.astype(f32)).astype(bf16)


PIECE = 640


def chunk_plan():
    kept = [(q, at) for q in range(IN_VMEM) for at in range(0, QUART, PIECE)]
    fetched = [(q, at) for q in range(IN_VMEM, 4) for at in range(0, QUART, PIECE)]
    order = []
    for n in range(max(len(kept), len(fetched))):
        order += kept[n : n + 1] + fetched[n : n + 1]
    return order, fetched


def apply_down(scaled, tiles, first):
    order, fetched = chunk_plan()
    slots = 3

    def body(*refs):
        s_ref, tile_refs, out_ref, held, sems = refs[0], refs[1:5], refs[5], refs[6], refs[7]

        def fetch(n):
            q, at = fetched[n]
            return pltpu.make_async_copy(
                tile_refs[q].at[pl.ds(at, PIECE), pl.ds(first, HALF)], held.at[n % slots], sems.at[n % slots]
            )

        for n in range(min(slots, len(fetched))):
            fetch(n).start()
        acc = None
        for q, at in order:
            if q < IN_VMEM:
                piece = tile_refs[q][at : at + PIECE, first : first + HALF]
            else:
                n = fetched.index((q, at))
                fetch(n).wait()
                piece = held[n % slots]
            s_hi, s_lo = two_terms(s_ref[:, q * QUART + at : q * QUART + at + PIECE])
            both = jnp.concatenate([s_hi, s_lo], axis=0)
            hi, lo = two_terms(piece)
            part = jnp.dot(both, hi, preferred_element_type=f32) + jnp.dot(both, lo, preferred_element_type=f32)
            if acc is None:
                out_ref[...] = part[0:16] + part[16:32]
                acc = True
            else:
                out_ref[...] += part[0:16] + part[16:32]
            if q >= IN_VMEM and n + slots < len(fetched):
                fetch(n + slots).start()

    return pl.pallas_call(
        body,
        in_specs=[WHOLE] + [WHOLE if q < IN_VMEM else ANY for q in range(4)],
        out_specs=WHOLE,
        out_shape=jax.ShapeDtypeStruct((TGT, HALF), f32),
        scratch_shapes=[pltpu.VMEM((slots, PIECE, HALF), f32), pltpu.SemaphoreType.DMA((slots,))],
        compiler_params=params(24),
        name="apply_down",
    )(scaled, *tiles)


def apply_across(scaled, tile, keep):
    step_rows = 640 if keep else 320

    def column_form(s_ref, held):
        s_hi, s_lo = two_terms(s_ref[...])
        held[...] = jnp.concatenate([s_hi.astype(f32), s_lo.astype(f32)], axis=0).T.astype(bf16)

    def product(piece, held):
        hi, lo = two_terms(piece)
        out = jnp.dot(hi, held[...], preferred_element_type=f32) + jnp.dot(lo, held[...], preferred_element_type=f32)
        out = out.T
        return out[0:16] + out[16:32]

    def kept_body(s_ref, tile_ref, out_ref, held):
        column_form(s_ref, held)
        for at in range(0, QUART, step_rows):
            out_ref[:, at : at + step_rows] = product(tile_ref[at : at + step_rows, :], held)

    def sent_body(s_ref, tile_ref, out_ref, held, ring, sems):
        def fetch(n):
            return pltpu.make_async_copy(
                tile_ref.at[pl.ds(n * step_rows, step_rows), :], ring.at[n % 3], sems.at[n % 3]
            )

        count = QUART // step_rows
        for n in range(3):
            fetch(n).start()
        column_form(s_ref, held)
        lines = []
        for n in range(count):
            fetch(n).wait()
            lines.append(product(ring[n % 3], held))
            if n + 3 < count:
                fetch(n + 3).start()
        out_ref[...] = jnp.concatenate(lines, axis=1)

    held = pltpu.VMEM((COLS, 32), bf16)
    return pl.pallas_call(
        kept_body if keep else sent_body,
        in_specs=[WHOLE, WHOLE if keep else ANY],
        out_specs=WHOLE,
        out_shape=jax.ShapeDtypeStruct((TGT, QUART), f32),
        scratch_shapes=[held]
        + ([] if keep else [pltpu.VMEM((3, step_rows, COLS), f32), pltpu.SemaphoreType.DMA((3,))]),
        compiler_params=params(24),
        name="apply_across",
    )(scaled, tile)


def swap(x, axis, by):
    n = 2 if axis == "k" else 4
    return lax.ppermute(x, axis, [(i, i ^ by) for i in range(n)])


X = ("xl", "xh")


def per_device(centres, targets, start_weights):
    pts, goal, start = centres.T, targets.T, start_weights.T
    ahead = goal + (1.0 - ridge_term) * start
    row_block = jnp.concatenate([pts, start], axis=0)
    col_block = jnp.concatenate([pts, ahead], axis=0)
    by_z = [row_block] + [swap(row_block, "z", m) for m in (1, 2, 3)]
    by_y = [col_block] + [swap(col_block, "y", m) for m in (1, 2, 3)]
    col_own = jnp.concatenate(by_y, axis=1)
    row_own = jnp.concatenate(by_z, axis=1)
    cols = jnp.concatenate([col_own[:FEAT], swap(col_own[:FEAT], "k", 1)], axis=1)
    rows = [row_own] + [swap(row_own, X, m) for m in (1, 2, 3)]

    tiles, tots = [], []
    for q in range(4):
        tile, tot = gram_quarter(rows[q], cols, q < IN_VMEM)
        tiles.append(tile)
        tots.append(tot)
    totals = jnp.stack(tots)
    from_z = [totals] + [swap(totals, "z", m) for m in (1, 2, 3)]
    totals = sum(
        jnp.stack([from_z[j][:, m ^ j] for m in range(4)], axis=1) for j in range(4)
    )
    from_x = [totals] + [swap(totals, X, m) for m in (1, 2, 3)]
    totals = sum(jnp.stack([from_x[j][m ^ j] for m in range(4)]) for j in range(4))
    own_tot = totals[0, 0][None, :]

    all_rows = jnp.concatenate([r[FEAT:] for r in rows], axis=1)
    scaled = all_rows / totals.reshape(1, 4 * QUART)

    other = apply_down(scaled, tiles, HALF)
    sent = swap(other, "k", 1)
    own = apply_down(scaled, tiles, 0) + sent
    packed = jnp.concatenate([own, jnp.pad(own_tot, ((0, 7), (0, QUART - BLK)))], axis=0)
    from_y = [packed] + [swap(packed, "y", m) for m in (1, 2, 3)]
    applied = 0.0
    for j in range(4):
        got = from_y[j][:TGT]
        applied = applied + jnp.concatenate(
            [got[:, (m ^ j) * BLK : ((m ^ j) + 1) * BLK] for m in range(4)], axis=1
        )
    col_tot = jnp.concatenate([from_y[j][TGT : TGT + 1, :BLK] for j in range(4)], axis=1)
    weighted = col_own[FEAT:] - applied
    scaled = weighted / col_tot
    scaled = jnp.concatenate([scaled, swap(scaled, "k", 1)], axis=1)

    moved = None
    total = None
    parts = {}
    for q in (1, 2, 3, 0):
        parts[q] = apply_across(scaled, tiles[q], q < IN_VMEM)
        if q:
            parts[q] = swap(parts[q], X, q)
    total = parts[0] + parts[1] + parts[2] + parts[3]
    applied = total[:, :BLK]
    for m in (1, 2, 3):
        applied = applied + swap(total[:, m * BLK : (m + 1) * BLK], "z", m)
    weighted = weighted[:, :BLK]
    residual = goal - applied - ridge_term * weighted
    weighted = weighted + residual
    return weighted.T, residual.T


def solution(mesh):
    fine = Mesh(mesh.devices.reshape(4, 2, 2, 4, 2), AXES)
    placed = P(AXES, None)
    return jax.shard_map(
        per_device, mesh=fine, in_specs=(placed,) * 3, out_specs=(placed,) * 2, check_vma=False
    )
```

```python
import jax
import jax.numpy as jnp
from jax import lax
from jax.experimental import pallas as pl
from jax.experimental.pallas import tpu as pltpu
from jax.sharding import Mesh, PartitionSpec as P

ITERS = 2

kernel_width = 2.0
soften = 0.01
ridge_term = 0.25

SCALE = 1.4426950408889634 / kernel_width
FLOOR = soften * SCALE * SCALE

f32 = jnp.float32
bf16 = jnp.bfloat16

AXES = ("y", "xl", "xh", "z", "k")
X = ("xl", "xh")
BLK = 320
FEAT = 64
TGT = 16
ROWS = FEAT + TGT
QUART = 4 * BLK
COLS = 8 * BLK
HALF = COLS // 2
KEPT = (True, True, False, False)

WHOLE = pl.BlockSpec(memory_space=pltpu.VMEM)
FAR = pl.BlockSpec(memory_space=pltpu.HBM)

NT = (((1,), (1,)), ((), ()))


def params(mib=12):
    return pltpu.CompilerParams(vmem_limit_bytes=mib << 20)


def tile_spec(q):
    return WHOLE if KEPT[q] else FAR


def tile_shape(q):
    return (pltpu.VMEM if KEPT[q] else pltpu.HBM)((QUART, COLS), f32)


def dense(*shape):
    return jax.ShapeDtypeStruct(shape, f32)


def two_terms(vals):
    high = vals.astype(bf16)
    return high, (vals - high.astype(f32)).astype(bf16)


def point_terms(block):
    high, low = two_terms(block.T * SCALE)
    kept = high.astype(f32) + low.astype(f32)
    return high, low, kept * kept


def row_setup(rows_ref, lhs, row_sq):
    for b in range(4):
        high, low, sq = point_terms(rows_ref[b * ROWS : b * ROWS + FEAT, :])
        here = slice(b * BLK, (b + 1) * BLK)
        lhs[here, :] = jnp.concatenate([high, high, low, low], axis=1) * jnp.asarray(2.0, bf16)
        row_sq[here, :] = jnp.sum(sq, axis=1, keepdims=True) + FLOOR


def col_setup(pair_refs, rhs, col_sq):
    lines = []
    for core in range(2):
        for m in range(4):
            block = pair_refs[m][core * ROWS : core * ROWS + FEAT, :]
            high, low, sq = point_terms(block)
            at = (core * 4 + m) * BLK
            rhs[at : at + BLK, :] = jnp.concatenate([high, low, high, low], axis=1)
            lines.append(jnp.sum(sq.T, axis=0, keepdims=True))
    col_sq[...] = jnp.concatenate(lines, axis=1)


def gram_part(lhs, rhs, row_sq, col_sq, at, width):
    cross = lax.dot_general(lhs[...], rhs[at : at + width, :], NT, preferred_element_type=f32)
    dist = jnp.maximum((row_sq[...] - cross) + col_sq[:, at : at + width], FLOOR)
    return jnp.exp2(-(dist * lax.rsqrt(dist)))


def fold_lanes(part):
    acc = part[:, 0:128]
    for at in range(128, part.shape[1], 128):
        acc = acc + part[:, at : at + 128]
    return acc


def put_totals(acc, tot_ref, q):
    line = jnp.sum(acc.T, axis=0, keepdims=True)
    for m in range(4):
        tot_ref[4 * q + m : 4 * q + m + 1, :] = line[:, m * BLK : (m + 1) * BLK]


STEP = 256
ROW_SCRATCH = [pltpu.VMEM((QUART, 256), bf16), pltpu.VMEM((QUART, 1), f32), pltpu.VMEM((QUART, 128), f32)]


def gram_first(rows, pairs):
    def body(rows_ref, p0, p1, p2, p3, tile_ref, tot_ref, rhs, col_sq, lhs, row_sq, acc):
        col_setup((p0, p1, p2, p3), rhs, col_sq)
        row_setup(rows_ref, lhs, row_sq)
        for at in range(0, COLS, STEP):
            part = gram_part(lhs, rhs, row_sq, col_sq, at, STEP)
            tile_ref[:, at : at + STEP] = part
            acc[...] = fold_lanes(part) if at == 0 else acc[...] + fold_lanes(part)
        put_totals(acc[...], tot_ref, 0)

    return pl.pallas_call(
        body,
        in_specs=[WHOLE] * 5,
        out_specs=[WHOLE] * 4,
        out_shape=[tile_shape(0), dense(16, BLK), jax.ShapeDtypeStruct((COLS, 256), bf16), dense(1, COLS)],
        scratch_shapes=ROW_SCRATCH,
        compiler_params=params(),
        name="gram_first",
    )(rows, *pairs)


def gram_rest(rows, rhs, col_sq, tile, tot):
    slots = 4

    def body(r1, r2, r3, rhs, col_sq, _, __, ___, tot_ref, t1, t2, t3, lhs, row_sq, acc, stage, sems):
        rows_of, tile_of = {1: r1, 2: r2, 3: r3}, {1: t1, 2: t2, 3: t3}
        sent = []

        def send(n):
            q, at = sent[n]
            return pltpu.make_async_copy(
                stage.at[n % slots], tile_of[q].at[:, pl.ds(at, STEP)], sems.at[n % slots]
            )

        waited = 0
        for q in (2, 3, 1):
            row_setup(rows_of[q], lhs, row_sq)
            for at in range(0, COLS, STEP):
                part = gram_part(lhs, rhs, row_sq, col_sq, at, STEP)
                acc[...] = fold_lanes(part) if at == 0 else acc[...] + fold_lanes(part)
                if KEPT[q]:
                    tile_of[q][:, at : at + STEP] = part
                    continue
                n = len(sent)
                if n >= slots:
                    send(n - slots).wait()
                    waited = n - slots + 1
                stage[n % slots] = part
                sent.append((q, at))
                send(n).start()
            put_totals(acc[...], tot_ref, q)
        for n in range(waited, len(sent)):
            send(n).wait()

    return pl.pallas_call(
        body,
        in_specs=[WHOLE] * 7,
        out_specs=[WHOLE, WHOLE] + [tile_spec(q) for q in (1, 2, 3)],
        out_shape=[tile_shape(0), dense(16, BLK)] + [tile_shape(q) for q in (1, 2, 3)],
        input_output_aliases={5: 0, 6: 1},
        scratch_shapes=ROW_SCRATCH + [pltpu.VMEM((slots, QUART, STEP), f32), pltpu.SemaphoreType.DMA((slots,))],
        compiler_params=params(),
        name="gram_rest",
    )(*rows, rhs, col_sq, tile, tot)


def add_totals(arrays, over_z):
    def body(a0, a1, a2, a3, out_ref):
        refs = (a0, a1, a2, a3)
        for r in range(16):
            line = None
            for j in range(4):
                at = r ^ j if over_z else r ^ (4 * j)
                term = refs[j][at : at + 1, :]
                line = term if line is None else line + term
            out_ref[r : r + 1, :] = line

    return pl.pallas_call(
        body,
        in_specs=[WHOLE] * 4,
        out_specs=WHOLE,
        out_shape=dense(16, BLK),
        compiler_params=params(),
        name="add_totals",
    )(*arrays)


CHUNK = 256
SLOTS = 4


def apply_down(rows, totals, tiles):
    order = []
    per = QUART // CHUNK
    for n in range(per):
        order += [(0, n), (2, n), (1, n), (3, n)]
    far = [item for item in order if not KEPT[item[0]]]

    def body(*refs):
        row_refs, tot_ref, tile_refs = refs[0:4], refs[4], refs[5:9]
        other_ref, own_ref = refs[9:11]
        weights, out, held, sems = refs[15:]

        def fetch(n):
            q, at = far[n]
            return pltpu.make_async_copy(
                tile_refs[q].at[pl.ds(at * CHUNK, CHUNK), :], held.at[n % SLOTS], sems.at[n % SLOTS]
            )

        for n in range(SLOTS):
            fetch(n).start()
        for q in range(4):
            blocks = [
                row_refs[q][b * ROWS + FEAT : (b + 1) * ROWS, :] / tot_ref[4 * q + b : 4 * q + b + 1, :]
                for b in range(4)
            ]
            high, low = two_terms(jnp.concatenate(blocks, axis=1))
            weights[:, q * QUART : (q + 1) * QUART] = jnp.concatenate([high, low], axis=0)
        first, n = True, 0
        for q, at in order:
            if KEPT[q]:
                piece = tile_refs[q][at * CHUNK : (at + 1) * CHUNK, :]
            else:
                fetch(n).wait()
                piece = held[n % SLOTS]
            start = q * QUART + at * CHUNK
            w = weights[:, start : start + CHUNK]
            hi, lo = two_terms(piece)
            part = jnp.dot(w, hi, preferred_element_type=f32) + jnp.dot(w, lo, preferred_element_type=f32)
            part = part[0:16] + part[16:32]
            if first:
                out[...] = part
                first = False
            else:
                out[...] += part
            if not KEPT[q]:
                if n + SLOTS < len(far):
                    fetch(n + SLOTS).start()
                n += 1
        own_ref[...] = out[:, 0:HALF]
        other_ref[...] = out[:, HALF:COLS]

    return pl.pallas_call(
        body,
        in_specs=[WHOLE] * 5 + [tile_spec(q) for q in range(4)],
        out_specs=[WHOLE] * 2 + [tile_spec(q) for q in range(4)],
        out_shape=[dense(TGT, HALF)] * 2 + [tile_shape(q) for q in range(4)],
        input_output_aliases={5 + q: 2 + q for q in range(4)},
        scratch_shapes=[
            pltpu.VMEM((32, 4 * QUART), bf16),
            pltpu.VMEM((TGT, COLS), f32),
            pltpu.VMEM((SLOTS, CHUNK, COLS), f32),
            pltpu.SemaphoreType.DMA((SLOTS,)),
        ],
        compiler_params=params(13),
        name="apply_down",
    )(*rows, totals, *tiles)


def pack(own, got, totals):
    def body(own_ref, got_ref, tot_ref, out_ref):
        out_ref[0:TGT, :] = own_ref[...] + got_ref[...]
        out_ref[TGT : TGT + 8, 0:BLK] = jnp.broadcast_to(tot_ref[0:1, :], (8, BLK))
        out_ref[TGT : TGT + 8, BLK:QUART] = jnp.zeros((8, QUART - BLK), f32)

    return pl.pallas_call(
        body,
        in_specs=[WHOLE] * 3,
        out_specs=WHOLE,
        out_shape=dense(TGT + 8, QUART),
        compiler_params=params(),
        name="pack",
    )(own, got, totals)


def first_update(packed, pairs):
    def body(a0, a1, a2, a3, p0, p1, p2, p3, weighted_ref, scaled_ref):
        refs, pair_refs = (a0, a1, a2, a3), (p0, p1, p2, p3)
        scaled = []
        for m in range(4):
            applied = None
            for j in range(4):
                at = (m ^ j) * BLK
                term = refs[j][0:TGT, at : at + BLK]
                applied = term if applied is None else applied + term
            weighted = pair_refs[m][FEAT:ROWS, :] - applied
            if m == 0:
                weighted_ref[...] = weighted
            scaled.append(weighted / refs[m][TGT : TGT + 1, 0:BLK])
        scaled_ref[...] = jnp.concatenate(scaled, axis=1)

    return pl.pallas_call(
        body,
        in_specs=[WHOLE] * 8,
        out_specs=[WHOLE] * 2,
        out_shape=[dense(TGT, BLK), dense(TGT, QUART)],
        compiler_params=params(),
        name="first_update",
    )(*packed, *pairs)


WIDE = 320


def apply_across(own, other, tiles, which):
    order = [(q, n) for q in which if KEPT[q] for n in range(QUART // WIDE)]
    far = [(q, n) for q in which if not KEPT[q] for n in range(QUART // WIDE)]
    lead = max(len(order) - len(far), 0)
    mixed = order[:lead]
    for n in range(max(len(order) - lead, len(far))):
        mixed += order[lead + n : lead + n + 1] + far[n : n + 1]
    slots = 3 if far else 1

    def body(*refs):
        own_ref, other_ref = refs[0:2]
        tile_refs = dict(zip(which, refs[2 : 2 + len(which)]))
        out_refs = dict(zip(which, refs[2 + len(which) : 2 + 2 * len(which)]))
        weights, held, sems = refs[2 + 3 * len(which) :]

        def fetch(n):
            q, at = far[n]
            return pltpu.make_async_copy(
                tile_refs[q].at[pl.ds(at * WIDE, WIDE), :], held.at[n % slots], sems.at[n % slots]
            )

        for n in range(min(slots, len(far))):
            fetch(n).start()
        for half, ref in ((0, own_ref), (1, other_ref)):
            high, low = two_terms(ref[...].T)
            weights[half * HALF : (half + 1) * HALF, :] = jnp.concatenate([high, low], axis=1)
        lines = {q: [] for q in which}
        n = 0
        for q, at in mixed:
            if KEPT[q]:
                piece = tile_refs[q][at * WIDE : (at + 1) * WIDE, :]
            else:
                fetch(n).wait()
                piece = held[n % slots]
            hi, lo = two_terms(piece)
            w = weights[...]
            part = jnp.dot(hi, w, preferred_element_type=f32) + jnp.dot(lo, w, preferred_element_type=f32)
            part = part.T
            lines[q].append(part[0:16] + part[16:32])
            if not KEPT[q]:
                if n + slots < len(far):
                    fetch(n + slots).start()
                n += 1
            if at == QUART // WIDE - 1:
                out_refs[q][...] = jnp.concatenate(lines[q], axis=1)

    count = len(which)
    return pl.pallas_call(
        body,
        in_specs=[WHOLE] * 2 + [tile_spec(q) for q in which],
        out_specs=[WHOLE] * count + [tile_spec(q) for q in which],
        out_shape=[dense(TGT, QUART)] * count + [tile_shape(q) for q in which],
        input_output_aliases={2 + n: count + n for n in range(count)},
        scratch_shapes=[
            pltpu.VMEM((COLS, 32), bf16),
            pltpu.VMEM((slots, WIDE, COLS) if far else (8, 128), f32),
            pltpu.SemaphoreType.DMA((slots,)),
        ],
        compiler_params=params(14),
        name="apply_across",
    )(own, other, *[tiles[q] for q in which])[:count]


def add_blocks(arrays):
    def body(a0, a1, a2, a3, o0, o1, o2, o3):
        total = (a0[...] + a1[...]) + (a2[...] + a3[...])
        for m, ref in enumerate((o0, o1, o2, o3)):
            ref[...] = total[:, m * BLK : (m + 1) * BLK]

    return pl.pallas_call(
        body,
        in_specs=[WHOLE] * 4,
        out_specs=[WHOLE] * 4,
        out_shape=[dense(TGT, BLK)] * 4,
        compiler_params=params(),
        name="add_blocks",
    )(*arrays)


def last_update(applied, weighted, goal):
    def body(a0, a1, a2, a3, weighted_ref, goal_ref, out_ref, residual_ref):
        applied = (a0[...] + a1[...]) + (a2[...] + a3[...])
        weighted = weighted_ref[...]
        residual = goal_ref[...] - applied - ridge_term * weighted
        residual_ref[...] = residual
        out_ref[...] = weighted + residual

    return pl.pallas_call(
        body,
        in_specs=[WHOLE] * 6,
        out_specs=[WHOLE] * 2,
        out_shape=[dense(TGT, BLK)] * 2,
        compiler_params=params(),
        name="last_update",
    )(*applied, weighted, goal)


def swap(x, axis, by):
    n = 2 if axis == "k" else 4
    return lax.ppermute(x, axis, [(i, i ^ by) for i in range(n)])


def spread(x, axis):
    return [x] + [swap(x, axis, m) for m in (1, 2, 3)]


def per_device(centres, targets, start_weights):
    pts, goal, start = centres.T, targets.T, start_weights.T
    ahead = goal + (1.0 - ridge_term) * start
    row_block = jnp.concatenate([pts, start], axis=0)
    col_block = jnp.concatenate([pts, ahead], axis=0)
    pairs = spread(jnp.concatenate([col_block, swap(col_block, "k", 1)], axis=0), "y")
    rows = spread(jnp.concatenate(spread(row_block, "z"), axis=0), X)

    tile, tot, rhs, col_sq = gram_first(rows[0], pairs)
    first, tot, *rest = gram_rest(rows[1:], rhs, col_sq, tile, tot)
    tiles = [first] + list(rest)
    tot = add_totals(spread(tot, "z"), True)
    tot = add_totals(spread(tot, X), False)

    other, own, *tiles = apply_down(rows, tot, tiles)
    packed = spread(pack(own, swap(other, "k", 1), tot), "y")
    weighted, scaled = first_update(packed, pairs)

    scaled_other = swap(scaled, "k", 1)
    parts = apply_across(scaled, scaled_other, tiles, (1, 2, 3))
    parts = [swap(part, X, q) for q, part in zip((1, 2, 3), parts)]
    parts += apply_across(scaled, scaled_other, tiles, (0,))
    blocks = add_blocks(parts)
    blocks = [blocks[0]] + [swap(blocks[m], "z", m) for m in (1, 2, 3)]
    weighted, residual = last_update(blocks, weighted, goal)
    return weighted.T, residual.T


def solution(mesh):
    fine = Mesh(mesh.devices.reshape(4, 2, 2, 4, 2), AXES)
    placed = P(AXES, None)
    return jax.shard_map(
        per_device, mesh=fine, in_specs=(placed,) * 3, out_specs=(placed,) * 2, check_vma=False
    )
```

```python
import jax
import jax.numpy as jnp
from jax import lax
from jax.experimental import pallas as pl
from jax.experimental.pallas import tpu as pltpu
from jax.sharding import Mesh, PartitionSpec as P

ITERS = 2

kernel_width = 2.0
soften = 0.01
ridge_term = 0.25

SCALE = 1.4426950408889634 / kernel_width
FLOOR = soften * SCALE * SCALE

f32 = jnp.float32
bf16 = jnp.bfloat16

AXES = ("y", "xl", "xh", "z", "k")
X = ("xl", "xh")
BLK = 320
FEAT = 64
TGT = 16
QUART = 4 * BLK
COLS = 8 * BLK
HALF = COLS // 2
KEPT = (False, True, True, False)

WHOLE = pl.BlockSpec(memory_space=pltpu.VMEM)
FAR = pl.BlockSpec(memory_space=pltpu.HBM)

NT = (((1,), (1,)), ((), ()))


def params(mib=12):
    return pltpu.CompilerParams(vmem_limit_bytes=mib << 20)


def tile_spec(q):
    return WHOLE if KEPT[q] else FAR


def tile_shape(q):
    return (pltpu.VMEM if KEPT[q] else pltpu.HBM)((QUART, COLS), f32)


def dense(*shape):
    return jax.ShapeDtypeStruct(shape, f32)


def two_terms(vals):
    high = vals.astype(bf16)
    return high, (vals - high.astype(f32)).astype(bf16)


LINES = 200
PTS = 160


def pack_values(out_ref, vals):
    out_ref[160:176, :] = vals[:, 0:128]
    out_ref[176:192, :] = vals[:, 128:256]
    out_ref[192:200, :] = jnp.concatenate([vals[0:8, 256:320], vals[8:16, 256:320]], axis=1)


def values_of(ref, at):
    tail = ref[at + 192 : at + 200, :]
    tail = jnp.concatenate([tail[:, 0:64], tail[:, 64:128]], axis=0)
    return jnp.concatenate([ref[at + 160 : at + 176, :], ref[at + 176 : at + 192, :], tail], axis=1)


def pack_blocks(pts, goal, start):
    def body(pts_far, goal_far, start_far, row_ref, col_ref, pts_ref, goal_ref, start_ref, sems):
        copies = [
            pltpu.make_async_copy(src, dst, sems.at[n])
            for n, (src, dst) in enumerate(((pts_far, pts_ref), (goal_far, goal_ref), (start_far, start_ref)))
        ]
        for copy in copies:
            copy.start()
        for copy in copies:
            copy.wait()
        flat = pts_ref[...].T
        both = jnp.concatenate([flat[0:PTS, :], flat[PTS:BLK, :]], axis=1)
        row_ref[0:PTS, :] = both
        col_ref[0:PTS, :] = both
        start = start_ref[...]
        pack_values(row_ref, start)
        pack_values(col_ref, goal_ref[...] + (1.0 - ridge_term) * start)

    return pl.pallas_call(
        body,
        in_specs=[pl.BlockSpec(memory_space=pl.ANY)] * 3,
        out_specs=[WHOLE] * 2,
        out_shape=[dense(LINES, 128)] * 2,
        scratch_shapes=[
            pltpu.VMEM((FEAT, BLK), f32),
            pltpu.VMEM((TGT, BLK), f32),
            pltpu.VMEM((TGT, BLK), f32),
            pltpu.SemaphoreType.DMA((3,)),
        ],
        compiler_params=params(),
        name="pack_blocks",
    )(pts, goal, start)


def join_blocks(by_z, by_y):
    def body(*refs):
        rows_ref, cols_ref = refs[8:]
        for m in range(4):
            rows_ref[m * LINES : (m + 1) * LINES, :] = refs[m][...]
            cols_ref[m * PTS : (m + 1) * PTS, :] = refs[4 + m][0:PTS, :]

    return pl.pallas_call(
        body,
        in_specs=[WHOLE] * 8,
        out_specs=[WHOLE] * 2,
        out_shape=[dense(4 * LINES, 128), dense(4 * PTS, 128)],
        compiler_params=params(),
        name="join_blocks",
    )(*by_z, *by_y)


def point_terms(lines):
    high, low = two_terms(lines * SCALE)
    kept = high.astype(f32) + low.astype(f32)
    return high, low, kept * kept


def row_setup(rows_ref, lhs, row_sq):
    for b in range(4):
        high, low, sq = point_terms(rows_ref[b * LINES : b * LINES + PTS, :])
        for half in range(2):
            at = b * BLK + half * PTS
            side = slice(64 * half, 64 * half + 64)
            hi, lo = high[:, side], low[:, side]
            lhs[at : at + PTS, :] = jnp.concatenate([hi, hi, lo, lo], axis=1) * jnp.asarray(2.0, bf16)
            row_sq[at : at + PTS, :] = jnp.sum(sq[:, side], axis=1, keepdims=True) + FLOOR


def col_setup(near_ref, far_ref, rhs, col_sq):
    lines = []
    for core, ref in enumerate((near_ref, far_ref)):
        for m in range(4):
            high, low, sq = point_terms(ref[m * PTS : (m + 1) * PTS, :])
            flat = sq.T
            for half in range(2):
                at = (core * 4 + m) * BLK + half * PTS
                side = slice(64 * half, 64 * half + 64)
                hi, lo = high[:, side], low[:, side]
                rhs[at : at + PTS, :] = jnp.concatenate([hi, lo, hi, lo], axis=1)
                lines.append(jnp.sum(flat[side, :], axis=0, keepdims=True))
    col_sq[...] = jnp.concatenate(lines, axis=1)


def gram_part(lhs, rhs, row_sq, col_sq, at, width):
    cross = lax.dot_general(lhs[...], rhs[at : at + width, :], NT, preferred_element_type=f32)
    dist = jnp.maximum((row_sq[...] - cross) + col_sq[:, at : at + width], FLOOR)
    return jnp.exp2(-(dist * lax.rsqrt(dist)))


def fold_lanes(part):
    acc = part[:, 0:128]
    for at in range(128, part.shape[1], 128):
        acc = acc + part[:, at : at + 128]
    return acc


def place():
    return (lax.axis_index("xl") * 2 + lax.axis_index("xh")) * 4 + lax.axis_index("z")


def put_totals(acc, tot_ref, q):
    line = jnp.sum(acc.T, axis=0, keepdims=True)
    here = place()
    for m in range(4):
        tot_ref[pl.ds(here ^ (4 * q + m), 1), :] = line[:, m * BLK : (m + 1) * BLK]


STEP = 256


def gram_kernel(which, rows, rhs, col_sq, tot, last, setup=None):
    slots = 4
    lead = [(q, n) for q in which if KEPT[q] for n in range(COLS // STEP)]
    far = [(q, n) for q in which if not KEPT[q] for n in range(COLS // STEP)]
    order = []
    for n in range(COLS // STEP):
        order += far[n : n + 1] + lead[n : n + 1]
    count = len(which)
    first = setup is not None

    def body(*refs):
        rows_of = dict(zip(which, refs[:count]))
        given, refs = refs[count : count + 3], refs[count + 3 :]
        if first:
            near_ref, far_ref, _ = given
            rhs, col_sq, tot_ref, refs = refs[0], refs[1], refs[2], refs[3:]
        else:
            rhs, col_sq, _ = given
            tot_ref, refs = refs[0], refs[1:]
        if last:
            out_ref, refs = refs[0], refs[1:]
        tile_of, refs = dict(zip(which, refs[:count])), refs[count:]
        own = {q: refs[3 * n : 3 * n + 3] for n, q in enumerate(which)}
        stage, sems = refs[3 * count :]
        sent = []

        def send(n):
            q, at = sent[n]
            return pltpu.make_async_copy(
                stage.at[n % slots], tile_of[q].at[:, pl.ds(at, STEP)], sems.at[n % slots]
            )

        if first:
            col_setup(near_ref, far_ref, rhs, col_sq)
        waited = 0
        for q, part_at in order:
            at = part_at * STEP
            lhs, row_sq, acc = own[q]
            if at == 0:
                row_setup(rows_of[q], lhs, row_sq)
            part = gram_part(lhs, rhs, row_sq, col_sq, at, STEP)
            acc[...] = fold_lanes(part) if at == 0 else acc[...] + fold_lanes(part)
            if KEPT[q]:
                tile_of[q][:, at : at + STEP] = part
            else:
                n = len(sent)
                if n >= slots:
                    send(n - slots).wait()
                    waited = n - slots + 1
                stage[n % slots] = part
                sent.append((q, at))
                send(n).start()
        for q in which:
            put_totals(own[q][2][...], tot_ref, q)
        if last:
            for n in range(16):
                out_ref[n] = tot_ref[...]
        for n in range(waited, len(sent)):
            send(n).wait()

    if first:
        given = [*setup, tot]
        made = [jax.ShapeDtypeStruct((COLS, 256), bf16), dense(1, COLS)]
    else:
        given, made = [rhs, col_sq, tot], []
    here = len(made)
    scratch = [pltpu.VMEM((QUART, 256), bf16), pltpu.VMEM((QUART, 1), f32), pltpu.VMEM((QUART, 128), f32)] * count
    scratch += [pltpu.VMEM((slots, QUART, STEP) if far else (8, 128), f32), pltpu.SemaphoreType.DMA((slots,))]
    out = made + [dense(16, BLK)] + ([dense(16, 16, BLK)] if last else [])
    return pl.pallas_call(
        body,
        in_specs=[WHOLE] * (count + 3),
        out_specs=[WHOLE] * len(out) + [tile_spec(q) for q in which],
        out_shape=out + [tile_shape(q) for q in which],
        input_output_aliases={count + 2: here},
        scratch_shapes=scratch,
        compiler_params=params(12 if last else 16),
        name="gram",
    )(*rows, *given)


CHUNK = 256
SLOTS = 4


def apply_down(rows, totals, tiles):
    order = []
    per = QUART // CHUNK
    for n in range(per):
        order += [(1, n), (0, n), (2, n), (3, n)]
    far = [item for item in order if not KEPT[item[0]]]

    def body(*refs):
        row_refs, parts_ref, tile_refs = refs[0:4], refs[4], refs[5:9]
        other_ref, own_ref, own_tot = refs[9:12]
        weights, out, tot_ref, held, sems = refs[16:]

        def fetch(n):
            q, at = far[n]
            return pltpu.make_async_copy(
                tile_refs[q].at[pl.ds(at * CHUNK, CHUNK), :], held.at[n % SLOTS], sems.at[n % SLOTS]
            )

        for n in range(SLOTS):
            fetch(n).start()
        here = place()
        total = parts_ref[0]
        for n in range(1, 16):
            total = total + parts_ref[n]
        tot_ref[...] = total
        own_tot[...] = jnp.broadcast_to(tot_ref[pl.ds(here, 1), :], (8, BLK))
        for q in range(4):
            blocks = [
                values_of(row_refs[q], b * LINES) / tot_ref[pl.ds(here ^ (4 * q + b), 1), :]
                for b in range(4)
            ]
            high, low = two_terms(jnp.concatenate(blocks, axis=1))
            weights[:, q * QUART : (q + 1) * QUART] = jnp.concatenate([high, low], axis=0)
        first, n = True, 0
        for q, at in order:
            if KEPT[q]:
                piece = tile_refs[q][at * CHUNK : (at + 1) * CHUNK, :]
            else:
                fetch(n).wait()
                piece = held[n % SLOTS]
            start = q * QUART + at * CHUNK
            w = weights[:, start : start + CHUNK]
            hi, lo = two_terms(piece)
            part = jnp.dot(w, hi, preferred_element_type=f32) + jnp.dot(w, lo, preferred_element_type=f32)
            part = part[0:16] + part[16:32]
            if first:
                out[...] = part
                first = False
            else:
                out[...] += part
            if not KEPT[q]:
                if n + SLOTS < len(far):
                    fetch(n + SLOTS).start()
                n += 1
        own_ref[...] = out[:, 0:HALF]
        other_ref[...] = out[:, HALF:COLS]

    return pl.pallas_call(
        body,
        in_specs=[WHOLE] * 5 + [tile_spec(q) for q in range(4)],
        out_specs=[WHOLE] * 3 + [tile_spec(q) for q in range(4)],
        out_shape=[dense(TGT, HALF)] * 2 + [dense(8, BLK)] + [tile_shape(q) for q in range(4)],
        input_output_aliases={5 + q: 3 + q for q in range(4)},
        scratch_shapes=[
            pltpu.VMEM((32, 4 * QUART), bf16),
            pltpu.VMEM((TGT, COLS), f32),
            pltpu.VMEM((16, BLK), f32),
            pltpu.VMEM((SLOTS, CHUNK, COLS), f32),
            pltpu.SemaphoreType.DMA((SLOTS,)),
        ],
        compiler_params=params(13),
        name="apply_down",
    )(*rows, totals, *tiles)


def pack(own, got, totals):
    def body(own_ref, got_ref, tot_ref, out_ref):
        out_ref[:, 0:QUART] = own_ref[...] + got_ref[...]
        out_ref[:, QUART : QUART + 128] = jnp.zeros((TGT, 128), f32)
        out_ref[0:1, QUART : QUART + 128] = tot_ref[0:1, 0:128]
        out_ref[1:2, QUART : QUART + 128] = tot_ref[0:1, 128:256]
        out_ref[2:3, QUART : QUART + 64] = tot_ref[0:1, 256:320]

    return pl.pallas_call(
        body,
        in_specs=[WHOLE] * 3,
        out_specs=WHOLE,
        out_shape=dense(TGT, QUART + 128),
        compiler_params=params(),
        name="pack",
    )(own, got, totals)


def first_update(packed, by_y):
    def body(a0, a1, a2, a3, b0, b1, b2, b3, weighted_ref, scaled_ref):
        refs, block_refs = (a0, a1, a2, a3), (b0, b1, b2, b3)
        scaled = []
        for m in range(4):
            applied = None
            for j in range(4):
                at = (m ^ j) * BLK
                term = refs[j][:, at : at + BLK]
                applied = term if applied is None else applied + term
            weighted = values_of(block_refs[m], 0) - applied
            if m == 0:
                weighted_ref[...] = weighted
            line = refs[m][0:8, QUART : QUART + 128]
            line = jnp.concatenate([line[0:1, :], line[1:2, :], line[2:3, 0:64]], axis=1)
            scaled.append(weighted / line)
        scaled_ref[...] = jnp.concatenate(scaled, axis=1)

    return pl.pallas_call(
        body,
        in_specs=[WHOLE] * 8,
        out_specs=[WHOLE] * 2,
        out_shape=[dense(TGT, BLK), dense(TGT, QUART)],
        compiler_params=params(),
        name="first_update",
    )(*packed, *by_y)


WIDE = 256


def apply_across(own, other, tiles, which):
    order = [(q, n) for q in which if KEPT[q] for n in range(QUART // WIDE)]
    far = [(q, n) for q in which if not KEPT[q] for n in range(QUART // WIDE)]
    lead = max(len(order) - len(far), 0)
    mixed = order[:lead]
    for n in range(max(len(order) - lead, len(far))):
        mixed += order[lead + n : lead + n + 1] + far[n : n + 1]
    slots = 4 if far else 1

    def body(*refs):
        own_ref, other_ref = refs[0:2]
        tile_refs = dict(zip(which, refs[2 : 2 + len(which)]))
        out_refs = dict(zip(which, refs[2 + len(which) : 2 + 2 * len(which)]))
        weights, held, sems = refs[2 + 3 * len(which) :]

        def fetch(n):
            q, at = far[n]
            return pltpu.make_async_copy(
                tile_refs[q].at[pl.ds(at * WIDE, WIDE), :], held.at[n % slots], sems.at[n % slots]
            )

        for n in range(min(slots, len(far))):
            fetch(n).start()
        for half, ref in ((0, own_ref), (1, other_ref)):
            high, low = two_terms(ref[...].T)
            weights[half * HALF : (half + 1) * HALF, :] = jnp.concatenate([high, low], axis=1)
        lines = {q: [] for q in which}
        n = 0
        for q, at in mixed:
            if KEPT[q]:
                piece = tile_refs[q][at * WIDE : (at + 1) * WIDE, :]
            else:
                fetch(n).wait()
                piece = held[n % slots]
            hi, lo = two_terms(piece)
            w = weights[...]
            part = jnp.dot(hi, w, preferred_element_type=f32) + jnp.dot(lo, w, preferred_element_type=f32)
            part = part.T
            lines[q].append(part[0:16] + part[16:32])
            if not KEPT[q]:
                if n + slots < len(far):
                    fetch(n + slots).start()
                n += 1
            if at == QUART // WIDE - 1:
                out_refs[q][...] = jnp.concatenate(lines[q], axis=1)

    count = len(which)
    return pl.pallas_call(
        body,
        in_specs=[WHOLE] * 2 + [tile_spec(q) for q in which],
        out_specs=[WHOLE] * count + [tile_spec(q) for q in which],
        out_shape=[dense(TGT, QUART)] * count + [tile_shape(q) for q in which],
        input_output_aliases={2 + n: count + n for n in range(count)},
        scratch_shapes=[
            pltpu.VMEM((COLS, 32), bf16),
            pltpu.VMEM((slots, WIDE, COLS) if far else (8, 128), f32),
            pltpu.SemaphoreType.DMA((slots,)),
        ],
        compiler_params=params(14),
        name="apply_across",
    )(own, other, *[tiles[q] for q in which])[:count]


def add_blocks(arrays):
    def body(a0, a1, a2, a3, o0, o1, o2, o3):
        total = (a0[...] + a1[...]) + (a2[...] + a3[...])
        for m, ref in enumerate((o0, o1, o2, o3)):
            ref[...] = total[:, m * BLK : (m + 1) * BLK]

    return pl.pallas_call(
        body,
        in_specs=[WHOLE] * 4,
        out_specs=[WHOLE] * 4,
        out_shape=[dense(TGT, BLK)] * 4,
        compiler_params=params(),
        name="add_blocks",
    )(*arrays)


def last_update(applied, weighted, goal):
    def body(a0, a1, a2, a3, weighted_ref, goal_ref, out_ref, residual_ref):
        applied = (a0[...] + a1[...]) + (a2[...] + a3[...])
        weighted = weighted_ref[...]
        residual = goal_ref[...] - applied - ridge_term * weighted
        residual_ref[...] = residual
        out_ref[...] = weighted + residual

    return pl.pallas_call(
        body,
        in_specs=[WHOLE] * 6,
        out_specs=[WHOLE] * 2,
        out_shape=[dense(TGT, BLK)] * 2,
        compiler_params=params(),
        name="last_update",
    )(*applied, weighted, goal)


def swap(x, axis, by):
    n = 2 if axis == "k" else 4
    return lax.ppermute(x, axis, [(i, i ^ by) for i in range(n)])


def spread(x, axis):
    return [x] + [swap(x, axis, m) for m in (1, 2, 3)]


def per_device(centres, targets, start_weights):
    pts, goal, start = centres.T, targets.T, start_weights.T
    row_block, col_block = pack_blocks(pts, goal, start)
    by_y = spread(col_block, "y")
    row_own, near = join_blocks(spread(row_block, "z"), by_y)
    far = swap(near, "k", 1)
    rows = spread(row_own, X)

    tot = jnp.zeros((16, BLK), f32)
    tiles = [None] * 4
    rhs, col_sq, tot, tiles[0] = gram_kernel((0,), rows[:1], None, None, tot, False, (near, far))
    tot, tiles[2], tiles[3] = gram_kernel((2, 3), rows[2:], rhs, col_sq, tot, False)
    tot, parts, tiles[1] = gram_kernel((1,), rows[1:2], rhs, col_sq, tot, True)
    parts = lax.all_to_all(parts, ("xl", "xh", "z"), 0, 0)

    other, own, tot, *tiles = apply_down(rows, parts, tiles)
    packed = spread(pack(own, swap(other, "k", 1), tot), "y")
    weighted, scaled = first_update(packed, by_y)

    scaled_other = swap(scaled, "k", 1)
    parts = apply_across(scaled, scaled_other, tiles, (1, 2, 3))
    parts = [swap(part, X, q) for q, part in zip((1, 2, 3), parts)]
    parts += apply_across(scaled, scaled_other, tiles, (0,))
    blocks = add_blocks(parts)
    blocks = [blocks[0]] + [swap(blocks[m], "z", m) for m in (1, 2, 3)]
    weighted, residual = last_update(blocks, weighted, goal)
    return weighted.T, residual.T


def solution(mesh):
    fine = Mesh(mesh.devices.reshape(4, 2, 2, 4, 2), AXES)
    placed = P(AXES, None)
    return jax.shard_map(
        per_device, mesh=fine, in_specs=(placed,) * 3, out_specs=(placed,) * 2, check_vma=False
    )
```

```python
import jax
import jax.numpy as jnp
from jax import lax
from jax.experimental import pallas as pl
from jax.experimental.pallas import tpu as pltpu
from jax.sharding import Mesh, PartitionSpec as P

ITERS = 2

kernel_width = 2.0
soften = 0.01
ridge_term = 0.25

SCALE = 1.4426950408889634 / kernel_width
FLOOR = soften * SCALE * SCALE

f32 = jnp.float32
bf16 = jnp.bfloat16

AXES = ("y", "xl", "xh", "z", "k")
X = ("xl", "xh")
BLK = 320
FEAT = 64
TGT = 16
QUART = 4 * BLK
COLS = 8 * BLK
HALF = COLS // 2
KEPT = (False, True, True, False)

WHOLE = pl.BlockSpec(memory_space=pltpu.VMEM)
FAR = pl.BlockSpec(memory_space=pltpu.HBM)

NT = (((1,), (1,)), ((), ()))


def params(mib=12):
    return pltpu.CompilerParams(vmem_limit_bytes=mib << 20)


def tile_spec(q):
    return WHOLE if KEPT[q] else FAR


def tile_shape(q):
    return (pltpu.VMEM if KEPT[q] else pltpu.HBM)((QUART, COLS), f32)


def dense(*shape):
    return jax.ShapeDtypeStruct(shape, f32)


def two_terms(vals):
    high = vals.astype(bf16)
    return high, (vals - high.astype(f32)).astype(bf16)


LINES = 200
PTS = 160
VALS = LINES - PTS


def pack_values(out_ref, vals):
    out_ref[160:176, :] = vals[:, 0:128]
    out_ref[176:192, :] = vals[:, 128:256]
    out_ref[192:200, :] = jnp.concatenate([vals[0:8, 256:320], vals[8:16, 256:320]], axis=1)


def values_of(ref, at):
    tail = ref[at + 32 : at + 40, :]
    tail = jnp.concatenate([tail[:, 0:64], tail[:, 64:128]], axis=0)
    return jnp.concatenate([ref[at : at + 16, :], ref[at + 16 : at + 32, :], tail], axis=1)


def pack_blocks(pts, goal, start):
    def body(pts_far, goal_far, start_far, row_ref, col_ref, pts_ref, goal_ref, start_ref, sems):
        copies = [
            pltpu.make_async_copy(src, dst, sems.at[n])
            for n, (src, dst) in enumerate(((pts_far, pts_ref), (goal_far, goal_ref), (start_far, start_ref)))
        ]
        for copy in copies:
            copy.start()
        for copy in copies:
            copy.wait()
        flat = pts_ref[...].T
        both = jnp.concatenate([flat[0:PTS, :], flat[PTS:BLK, :]], axis=1)
        row_ref[0:PTS, :] = both
        col_ref[0:PTS, :] = both
        start = start_ref[...]
        pack_values(row_ref, start)
        pack_values(col_ref, goal_ref[...] + (1.0 - ridge_term) * start)

    return pl.pallas_call(
        body,
        in_specs=[pl.BlockSpec(memory_space=pl.ANY)] * 3,
        out_specs=[WHOLE] * 2,
        out_shape=[dense(LINES, 128)] * 2,
        scratch_shapes=[
            pltpu.VMEM((FEAT, BLK), f32),
            pltpu.VMEM((TGT, BLK), f32),
            pltpu.VMEM((TGT, BLK), f32),
            pltpu.SemaphoreType.DMA((3,)),
        ],
        compiler_params=params(),
        name="pack_blocks",
    )(pts, goal, start)


def join_pair(own, got):
    def body(own_ref, got_ref, out_ref):
        out_ref[0:LINES, :] = own_ref[...]
        out_ref[LINES : 2 * LINES, :] = got_ref[...]

    return pl.pallas_call(
        body,
        in_specs=[WHOLE] * 2,
        out_specs=WHOLE,
        out_shape=dense(2 * LINES, 128),
        compiler_params=params(),
        name="join_pair",
    )(own, got)


PAIRS = ((0, 0), (0, 1), (1, 1), (1, 0))


def join_rows(own, got):
    def body(own_ref, got_ref, out_ref):
        for m, (pair, at) in enumerate(PAIRS):
            ref = (own_ref, got_ref)[pair]
            out_ref[m * LINES : (m + 1) * LINES, :] = ref[at * LINES : (at + 1) * LINES, :]

    return pl.pallas_call(
        body,
        in_specs=[WHOLE] * 2,
        out_specs=WHOLE,
        out_shape=dense(4 * LINES, 128),
        compiler_params=params(),
        name="join_rows",
    )(own, got)


def join_cols(own, got):
    def body(own_ref, got_ref, near_ref, ahead_ref):
        for m, (pair, at) in enumerate(PAIRS):
            ref, at = (own_ref, got_ref)[pair], at * LINES
            near_ref[m * PTS : (m + 1) * PTS, :] = ref[at : at + PTS, :]
            ahead_ref[m * VALS : (m + 1) * VALS, :] = ref[at + PTS : at + LINES, :]

    return pl.pallas_call(
        body,
        in_specs=[WHOLE] * 2,
        out_specs=[WHOLE] * 2,
        out_shape=[dense(4 * PTS, 128), dense(4 * VALS, 128)],
        compiler_params=params(),
        name="join_cols",
    )(own, got)


def point_terms(lines):
    high, low = two_terms(lines * SCALE)
    kept = high.astype(f32) + low.astype(f32)
    return high, low, kept * kept


def row_setup(rows_ref, lhs, row_sq):
    for b in range(4):
        high, low, sq = point_terms(rows_ref[b * LINES : b * LINES + PTS, :])
        for half in range(2):
            at = b * BLK + half * PTS
            side = slice(64 * half, 64 * half + 64)
            hi, lo = high[:, side], low[:, side]
            lhs[at : at + PTS, :] = jnp.concatenate([hi, hi, lo, lo], axis=1) * jnp.asarray(2.0, bf16)
            total = jnp.sum(sq[:, side], axis=1, keepdims=True) + FLOOR
            row_sq[at : at + PTS, :] = jnp.broadcast_to(total, (PTS, 128))


def col_setup(near_ref, far_ref, rhs, col_sq):
    lines = []
    for core, ref in enumerate((near_ref, far_ref)):
        for m in range(4):
            high, low, sq = point_terms(ref[m * PTS : (m + 1) * PTS, :])
            flat = sq.T
            for half in range(2):
                at = (core * 4 + m) * BLK + half * PTS
                side = slice(64 * half, 64 * half + 64)
                hi, lo = high[:, side], low[:, side]
                rhs[at : at + PTS, :] = jnp.concatenate([hi, lo, hi, lo], axis=1)
                lines.append(jnp.sum(flat[side, :], axis=0, keepdims=True))
    col_sq[...] = jnp.concatenate(lines, axis=1)


def gram_part(lhs, rhs, row_sq, col_sq, at, out, to):
    cross = lax.dot_general(lhs[...], rhs[at : at + STEP, :], NT, preferred_element_type=f32)
    sums = None
    for lane in range(0, STEP, 128):
        minus = (cross[:, lane : lane + 128] - row_sq[...]) - col_sq[:, at + lane : at + lane + 128]
        part = jnp.exp2(minus * lax.rsqrt(jnp.abs(minus)))
        out[:, to + lane : to + lane + 128] = part
        sums = part if sums is None else sums + part
    return sums


def place():
    return (lax.axis_index("xl") * 2 + lax.axis_index("xh")) * 4 + lax.axis_index("z")


def put_totals(acc, tot_ref, q):
    line = jnp.sum(acc.T, axis=0, keepdims=True)
    here = place()
    for m in range(4):
        tot_ref[pl.ds(here ^ (4 * q + m), 1), :] = line[:, m * BLK : (m + 1) * BLK]


STEP = 256


def gram_kernel(which, rows, rhs, col_sq, tot, last, setup=None):
    slots = 4
    lead = [(q, n) for q in which if KEPT[q] for n in range(COLS // STEP)]
    far = [(q, n) for q in which if not KEPT[q] for n in range(COLS // STEP)]
    order = []
    for n in range(max(len(far), len(lead))):
        order += far[n : n + 1] + lead[n : n + 1]
    count = len(which)
    first = setup is not None

    def body(*refs):
        rows_of = dict(zip(which, refs[:count]))
        given, refs = refs[count : count + 3], refs[count + 3 :]
        if first:
            near_ref, far_ref, _ = given
            rhs, col_sq, tot_ref, refs = refs[0], refs[1], refs[2], refs[3:]
        else:
            rhs, col_sq, _ = given
            tot_ref, refs = refs[0], refs[1:]
        if last:
            out_ref, refs = refs[0], refs[1:]
        tile_of, refs = dict(zip(which, refs[:count])), refs[count:]
        own = {q: refs[3 * n : 3 * n + 3] for n, q in enumerate(which)}
        stage, sems = refs[3 * count :]
        sent = []

        def send(n):
            q, at = sent[n]
            return pltpu.make_async_copy(
                stage.at[n % slots], tile_of[q].at[:, pl.ds(at, STEP)], sems.at[n % slots]
            )

        if first:
            col_setup(near_ref, far_ref, rhs, col_sq)
        waited = 0
        for q, part_at in order:
            at = part_at * STEP
            lhs, row_sq, acc = own[q]
            if at == 0:
                row_setup(rows_of[q], lhs, row_sq)
            n = len(sent)
            if not KEPT[q] and n >= slots:
                send(n - slots).wait()
                waited = n - slots + 1
            out, to = (tile_of[q], at) if KEPT[q] else (stage.at[n % slots], 0)
            sums = gram_part(lhs, rhs, row_sq, col_sq, at, out, to)
            acc[...] = sums if at == 0 else acc[...] + sums
            if not KEPT[q]:
                sent.append((q, at))
                send(n).start()
        for q in which:
            put_totals(own[q][2][...], tot_ref, q)
        if last:
            for n in range(16):
                out_ref[n] = tot_ref[...]
        for n in range(waited, len(sent)):
            send(n).wait()

    if first:
        given = [*setup, tot]
        made = [jax.ShapeDtypeStruct((COLS, 256), bf16), dense(1, COLS)]
    else:
        given, made = [rhs, col_sq, tot], []
    here = len(made)
    scratch = [pltpu.VMEM((QUART, 256), bf16), pltpu.VMEM((QUART, 128), f32), pltpu.VMEM((QUART, 128), f32)] * count
    scratch += [pltpu.VMEM((slots, QUART, STEP) if far else (8, 128), f32), pltpu.SemaphoreType.DMA((slots,))]
    out = made + [dense(16, BLK)] + ([dense(16, 16, BLK)] if last else [])
    return pl.pallas_call(
        body,
        in_specs=[WHOLE] * (count + 3),
        out_specs=[WHOLE] * len(out) + [tile_spec(q) for q in which],
        out_shape=out + [tile_shape(q) for q in which],
        input_output_aliases={count + 2: here},
        scratch_shapes=scratch,
        compiler_params=params(12 if last else 16),
        name="gram",
    )(*rows, *given)


CHUNK = 256
SLOTS = 4


def apply_down(rows, totals, tiles):
    order = []
    per = QUART // CHUNK
    for n in range(per):
        order += [(1, n), (0, n), (2, n), (3, n)]
    far = [item for item in order if not KEPT[item[0]]]

    def body(*refs):
        row_refs, parts_ref, tile_refs = refs[0:4], refs[4], refs[5:9]
        other_ref, own_ref, own_tot = refs[9:12]
        weights, out, tot_ref, held, sems = refs[16:]

        def fetch(n):
            q, at = far[n]
            return pltpu.make_async_copy(
                tile_refs[q].at[pl.ds(at * CHUNK, CHUNK), :], held.at[n % SLOTS], sems.at[n % SLOTS]
            )

        for n in range(SLOTS):
            fetch(n).start()
        here = place()
        total = parts_ref[0]
        for n in range(1, 16):
            total = total + parts_ref[n]
        tot_ref[...] = total
        own_tot[...] = jnp.broadcast_to(tot_ref[pl.ds(here, 1), :], (8, BLK))
        for q in range(4):
            blocks = [
                values_of(row_refs[q], b * LINES + PTS) / tot_ref[pl.ds(here ^ (4 * q + b), 1), :]
                for b in range(4)
            ]
            high, low = two_terms(jnp.concatenate(blocks, axis=1))
            weights[:, q * QUART : (q + 1) * QUART] = jnp.concatenate([high, low], axis=0)
        first, n = True, 0
        for q, at in order:
            if KEPT[q]:
                piece = tile_refs[q][at * CHUNK : (at + 1) * CHUNK, :]
            else:
                fetch(n).wait()
                piece = held[n % SLOTS]
            start = q * QUART + at * CHUNK
            w = weights[:, start : start + CHUNK]
            hi, lo = two_terms(piece)
            part = jnp.dot(w, hi, preferred_element_type=f32) + jnp.dot(w, lo, preferred_element_type=f32)
            part = part[0:16] + part[16:32]
            if first:
                out[...] = part
                first = False
            else:
                out[...] += part
            if not KEPT[q]:
                if n + SLOTS < len(far):
                    fetch(n + SLOTS).start()
                n += 1
        own_ref[...] = out[:, 0:HALF]
        other_ref[...] = out[:, HALF:COLS]

    return pl.pallas_call(
        body,
        in_specs=[WHOLE] * 5 + [tile_spec(q) for q in range(4)],
        out_specs=[WHOLE] * 3 + [tile_spec(q) for q in range(4)],
        out_shape=[dense(TGT, HALF)] * 2 + [dense(8, BLK)] + [tile_shape(q) for q in range(4)],
        input_output_aliases={5 + q: 3 + q for q in range(4)},
        scratch_shapes=[
            pltpu.VMEM((32, 4 * QUART), bf16),
            pltpu.VMEM((TGT, COLS), f32),
            pltpu.VMEM((16, BLK), f32),
            pltpu.VMEM((SLOTS, CHUNK, COLS), f32),
            pltpu.SemaphoreType.DMA((SLOTS,)),
        ],
        compiler_params=params(13),
        name="apply_down",
    )(*rows, totals, *tiles)


def pack(own, got, totals):
    def body(own_ref, got_ref, tot_ref, out_ref):
        out_ref[:, 0:QUART] = own_ref[...] + got_ref[...]
        out_ref[:, QUART : QUART + 128] = jnp.zeros((TGT, 128), f32)
        out_ref[0:1, QUART : QUART + 128] = tot_ref[0:1, 0:128]
        out_ref[1:2, QUART : QUART + 128] = tot_ref[0:1, 128:256]
        out_ref[2:3, QUART : QUART + 64] = tot_ref[0:1, 256:320]

    return pl.pallas_call(
        body,
        in_specs=[WHOLE] * 3,
        out_specs=WHOLE,
        out_shape=dense(TGT, QUART + 128),
        compiler_params=params(),
        name="pack",
    )(own, got, totals)


def first_update(packed, ahead):
    def body(a0, a1, a2, a3, ahead_ref, weighted_ref, scaled_ref):
        refs = (a0, a1, a2, a3)
        scaled = []
        for m in range(4):
            applied = None
            for j in range(4):
                at = (m ^ j) * BLK
                term = refs[j][:, at : at + BLK]
                applied = term if applied is None else applied + term
            weighted = values_of(ahead_ref, m * VALS) - applied
            if m == 0:
                weighted_ref[...] = weighted
            line = refs[m][0:8, QUART : QUART + 128]
            line = jnp.concatenate([line[0:1, :], line[1:2, :], line[2:3, 0:64]], axis=1)
            scaled.append(weighted / line)
        scaled_ref[...] = jnp.concatenate(scaled, axis=1)

    return pl.pallas_call(
        body,
        in_specs=[WHOLE] * 5,
        out_specs=[WHOLE] * 2,
        out_shape=[dense(TGT, BLK), dense(TGT, QUART)],
        compiler_params=params(),
        name="first_update",
    )(*packed, ahead)


WIDE = 256


def apply_across(own, other, tiles, which):
    order = [(q, n) for q in which if KEPT[q] for n in range(QUART // WIDE)]
    far = [(q, n) for q in which if not KEPT[q] for n in range(QUART // WIDE)]
    lead = max(len(order) - len(far), 0)
    mixed = order[:lead]
    for n in range(max(len(order) - lead, len(far))):
        mixed += order[lead + n : lead + n + 1] + far[n : n + 1]
    slots = 4 if far else 1

    def body(*refs):
        own_ref, other_ref = refs[0:2]
        tile_refs = dict(zip(which, refs[2 : 2 + len(which)]))
        out_refs = dict(zip(which, refs[2 + len(which) : 2 + 2 * len(which)]))
        weights, held, sems = refs[2 + 3 * len(which) :]

        def fetch(n):
            q, at = far[n]
            return pltpu.make_async_copy(
                tile_refs[q].at[pl.ds(at * WIDE, WIDE), :], held.at[n % slots], sems.at[n % slots]
            )

        for n in range(min(slots, len(far))):
            fetch(n).start()
        for half, ref in ((0, own_ref), (1, other_ref)):
            high, low = two_terms(ref[...].T)
            weights[half * HALF : (half + 1) * HALF, :] = jnp.concatenate([high, low], axis=1)
        lines = {q: [] for q in which}
        n = 0
        for q, at in mixed:
            if KEPT[q]:
                piece = tile_refs[q][at * WIDE : (at + 1) * WIDE, :]
            else:
                fetch(n).wait()
                piece = held[n % slots]
            hi, lo = two_terms(piece)
            w = weights[...]
            part = jnp.dot(hi, w, preferred_element_type=f32) + jnp.dot(lo, w, preferred_element_type=f32)
            part = part.T
            lines[q].append(part[0:16] + part[16:32])
            if not KEPT[q]:
                if n + slots < len(far):
                    fetch(n + slots).start()
                n += 1
            if at == QUART // WIDE - 1:
                out_refs[q][...] = jnp.concatenate(lines[q], axis=1)

    count = len(which)
    return pl.pallas_call(
        body,
        in_specs=[WHOLE] * 2 + [tile_spec(q) for q in which],
        out_specs=[WHOLE] * count + [tile_spec(q) for q in which],
        out_shape=[dense(TGT, QUART)] * count + [tile_shape(q) for q in which],
        input_output_aliases={2 + n: count + n for n in range(count)},
        scratch_shapes=[
            pltpu.VMEM((COLS, 32), bf16),
            pltpu.VMEM((slots, WIDE, COLS) if far else (8, 128), f32),
            pltpu.SemaphoreType.DMA((slots,)),
        ],
        compiler_params=params(14),
        name="apply_across",
    )(own, other, *[tiles[q] for q in which])[:count]


def add_blocks(arrays):
    def body(a0, a1, a2, a3, o0, o1, o2, o3):
        total = (a0[...] + a1[...]) + (a2[...] + a3[...])
        for m, ref in enumerate((o0, o1, o2, o3)):
            ref[...] = total[:, m * BLK : (m + 1) * BLK]

    return pl.pallas_call(
        body,
        in_specs=[WHOLE] * 4,
        out_specs=[WHOLE] * 4,
        out_shape=[dense(TGT, BLK)] * 4,
        compiler_params=params(),
        name="add_blocks",
    )(*arrays)


def last_update(applied, weighted, goal):
    def body(a0, a1, a2, a3, weighted_ref, goal_ref, out_ref, residual_ref):
        applied = (a0[...] + a1[...]) + (a2[...] + a3[...])
        weighted = weighted_ref[...]
        residual = goal_ref[...] - applied - ridge_term * weighted
        residual_ref[...] = residual
        out_ref[...] = weighted + residual

    return pl.pallas_call(
        body,
        in_specs=[WHOLE] * 6,
        out_specs=[WHOLE] * 2,
        out_shape=[dense(TGT, BLK)] * 2,
        compiler_params=params(),
        name="last_update",
    )(*applied, weighted, goal)


def swap(x, axis, by):
    n = 2 if axis == "k" else 4
    return lax.ppermute(x, axis, [(i, i ^ by) for i in range(n)])


def spread(x, axis):
    return [x] + [swap(x, axis, m) for m in (1, 2, 3)]


def per_device(centres, targets, start_weights):
    pts, goal, start = centres.T, targets.T, start_weights.T
    row_block, col_block = pack_blocks(pts, goal, start)
    row_pair = join_pair(row_block, swap(row_block, "z", 1))
    col_pair = join_pair(col_block, swap(col_block, "y", 1))
    row_own = join_rows(row_pair, swap(row_pair, "z", 3))
    near, ahead = join_cols(col_pair, swap(col_pair, "y", 3))
    far = swap(near, "k", 1)
    rows = spread(row_own, X)

    tot = jnp.zeros((16, BLK), f32)
    tiles = [None] * 4
    rhs, col_sq, tot, tiles[0] = gram_kernel((0,), rows[:1], None, None, tot, False, (near, far))
    tot, tiles[2], tiles[3] = gram_kernel((2, 3), rows[2:], rhs, col_sq, tot, False)
    tot, parts, tiles[1] = gram_kernel((1,), rows[1:2], rhs, col_sq, tot, True)
    parts = lax.all_to_all(parts, ("xl", "xh", "z"), 0, 0)

    other, own, tot, *tiles = apply_down(rows, parts, tiles)
    packed = spread(pack(own, swap(other, "k", 1), tot), "y")
    weighted, scaled = first_update(packed, ahead)

    scaled_other = swap(scaled, "k", 1)
    parts = apply_across(scaled, scaled_other, tiles, (1, 2, 3))
    parts = [swap(part, X, q) for q, part in zip((1, 2, 3), parts)]
    parts += apply_across(scaled, scaled_other, tiles, (0,))
    blocks = add_blocks(parts)
    blocks = [blocks[0]] + [swap(blocks[m], "z", m) for m in (1, 2, 3)]
    weighted, residual = last_update(blocks, weighted, goal)
    return weighted.T, residual.T


def solution(mesh):
    fine = Mesh(mesh.devices.reshape(4, 2, 2, 4, 2), AXES)
    placed = P(AXES, None)
    return jax.shard_map(
        per_device, mesh=fine, in_specs=(placed,) * 3, out_specs=(placed,) * 2, check_vma=False
    )
```

```python
import jax
import jax.numpy as jnp
from jax import lax
from jax.experimental import pallas as pl
from jax.experimental.pallas import tpu as pltpu
from jax.sharding import Mesh, PartitionSpec as P

ITERS = 2

kernel_width = 2.0
soften = 0.01
ridge_term = 0.25

SCALE = 1.4426950408889634 / kernel_width
FLOOR = soften * SCALE * SCALE

f32 = jnp.float32
bf16 = jnp.bfloat16

AXES = ("y", "xl", "xh", "z", "k")
X = ("xl", "xh")
BLK = 320
FEAT = 64
TGT = 16
QUART = 4 * BLK
COLS = 8 * BLK
HALF = COLS // 2
PIECES = (
    (0, 0, 256, True),
    (0, 256, 1024, False),
    (1, 0, 1280, True),
    (2, 0, 1280, True),
    (3, 0, 1280, False),
)
UNIT = 256


def pieces_of(which):
    return [p for p, piece in enumerate(PIECES) if piece[0] in which]


def units_of(which, kept):
    return [(p, at) for p in pieces_of(which) if PIECES[p][3] == kept for at in range(0, PIECES[p][2], UNIT)]


def in_turn(lead, rest):
    order = []
    for n in range(max(len(lead), len(rest))):
        order += lead[n : n + 1] + rest[n : n + 1]
    return order

WHOLE = pl.BlockSpec(memory_space=pltpu.VMEM)
FAR = pl.BlockSpec(memory_space=pltpu.HBM)

NT = (((1,), (1,)), ((), ()))


def params(mib=12):
    return pltpu.CompilerParams(vmem_limit_bytes=mib << 20)


def tile_spec(p):
    return WHOLE if PIECES[p][3] else FAR


def tile_shape(p):
    return (pltpu.VMEM if PIECES[p][3] else pltpu.HBM)((PIECES[p][2], COLS), f32)


def dense(*shape):
    return jax.ShapeDtypeStruct(shape, f32)


def two_terms(vals):
    high = vals.astype(bf16)
    return high, (vals - high.astype(f32)).astype(bf16)


LINES = 200
PTS = 160
VALS = LINES - PTS


def pack_values(out_ref, vals):
    out_ref[160:176, :] = vals[:, 0:128]
    out_ref[176:192, :] = vals[:, 128:256]
    out_ref[192:200, :] = jnp.concatenate([vals[0:8, 256:320], vals[8:16, 256:320]], axis=1)


def values_of(ref, at):
    tail = ref[at + 32 : at + 40, :]
    tail = jnp.concatenate([tail[:, 0:64], tail[:, 64:128]], axis=0)
    return jnp.concatenate([ref[at : at + 16, :], ref[at + 16 : at + 32, :], tail], axis=1)


def pack_blocks(pts, goal, start):
    def body(pts_far, goal_far, start_far, row_ref, col_ref, pts_ref, goal_ref, start_ref, sems):
        copies = [
            pltpu.make_async_copy(src, dst, sems.at[n])
            for n, (src, dst) in enumerate(((pts_far, pts_ref), (goal_far, goal_ref), (start_far, start_ref)))
        ]
        for copy in copies:
            copy.start()
        for copy in copies:
            copy.wait()
        flat = pts_ref[...].T
        both = jnp.concatenate([flat[0:PTS, :], flat[PTS:BLK, :]], axis=1)
        row_ref[0:PTS, :] = both
        col_ref[0:PTS, :] = both
        start = start_ref[...]
        pack_values(row_ref, start)
        pack_values(col_ref, goal_ref[...] + (1.0 - ridge_term) * start)

    return pl.pallas_call(
        body,
        in_specs=[pl.BlockSpec(memory_space=pl.ANY)] * 3,
        out_specs=[WHOLE] * 2,
        out_shape=[dense(LINES, 128)] * 2,
        scratch_shapes=[
            pltpu.VMEM((FEAT, BLK), f32),
            pltpu.VMEM((TGT, BLK), f32),
            pltpu.VMEM((TGT, BLK), f32),
            pltpu.SemaphoreType.DMA((3,)),
        ],
        compiler_params=params(),
        name="pack_blocks",
    )(pts, goal, start)


def join_pair(own, got):
    def body(own_ref, got_ref, out_ref):
        out_ref[0:LINES, :] = own_ref[...]
        out_ref[LINES : 2 * LINES, :] = got_ref[...]

    return pl.pallas_call(
        body,
        in_specs=[WHOLE] * 2,
        out_specs=WHOLE,
        out_shape=dense(2 * LINES, 128),
        compiler_params=params(),
        name="join_pair",
    )(own, got)


PAIRS = ((0, 0), (0, 1), (1, 1), (1, 0))


def join_rows(own, got):
    def body(own_ref, got_ref, out_ref):
        for m, (pair, at) in enumerate(PAIRS):
            ref = (own_ref, got_ref)[pair]
            out_ref[m * LINES : (m + 1) * LINES, :] = ref[at * LINES : (at + 1) * LINES, :]

    return pl.pallas_call(
        body,
        in_specs=[WHOLE] * 2,
        out_specs=WHOLE,
        out_shape=dense(4 * LINES, 128),
        compiler_params=params(),
        name="join_rows",
    )(own, got)


def join_cols(own, got):
    def body(own_ref, got_ref, near_ref, ahead_ref):
        for m, (pair, at) in enumerate(PAIRS):
            ref, at = (own_ref, got_ref)[pair], at * LINES
            near_ref[m * PTS : (m + 1) * PTS, :] = ref[at : at + PTS, :]
            ahead_ref[m * VALS : (m + 1) * VALS, :] = ref[at + PTS : at + LINES, :]

    return pl.pallas_call(
        body,
        in_specs=[WHOLE] * 2,
        out_specs=[WHOLE] * 2,
        out_shape=[dense(4 * PTS, 128), dense(4 * VALS, 128)],
        compiler_params=params(),
        name="join_cols",
    )(own, got)


def point_terms(lines):
    high, low = two_terms(lines * SCALE)
    kept = high.astype(f32) + low.astype(f32)
    return high, low, kept * kept


def row_setup(rows_ref, lhs, row_sq):
    for b in range(4):
        high, low, sq = point_terms(rows_ref[b * LINES : b * LINES + PTS, :])
        for half in range(2):
            at = b * BLK + half * PTS
            side = slice(64 * half, 64 * half + 64)
            hi, lo = high[:, side], low[:, side]
            lhs[at : at + PTS, :] = jnp.concatenate([hi, hi, lo, lo], axis=1) * jnp.asarray(2.0, bf16)
            total = jnp.sum(sq[:, side], axis=1, keepdims=True) + FLOOR
            row_sq[at : at + PTS, :] = jnp.broadcast_to(total, (PTS, 128))


def col_setup(near_ref, far_ref, rhs, col_sq):
    lines = []
    for core, ref in enumerate((near_ref, far_ref)):
        for m in range(4):
            high, low, sq = point_terms(ref[m * PTS : (m + 1) * PTS, :])
            flat = sq.T
            for half in range(2):
                at = (core * 4 + m) * BLK + half * PTS
                side = slice(64 * half, 64 * half + 64)
                hi, lo = high[:, side], low[:, side]
                rhs[at : at + PTS, :] = jnp.concatenate([hi, lo, hi, lo], axis=1)
                lines.append(jnp.sum(flat[side, :], axis=0, keepdims=True))
    col_sq[...] = jnp.concatenate(lines, axis=1)


def gram_part(lhs, rhs, row_sq, col_sq, at, outs):
    cross = lax.dot_general(lhs[...], rhs[at : at + STEP, :], NT, preferred_element_type=f32)
    sums = None
    for lane in range(0, STEP, 128):
        minus = (cross[:, lane : lane + 128] - row_sq[...]) - col_sq[:, at + lane : at + lane + 128]
        part = jnp.exp2(minus * lax.rsqrt(jnp.abs(minus)))
        for out, start, rows, to in outs:
            out[0:rows, to + lane : to + lane + 128] = part[start : start + rows, :]
        sums = part if sums is None else sums + part
    return sums


def place():
    return (lax.axis_index("xl") * 2 + lax.axis_index("xh")) * 4 + lax.axis_index("z")


def put_totals(acc, tot_ref, q):
    line = jnp.sum(acc.T, axis=0, keepdims=True)
    here = place()
    for m in range(4):
        tot_ref[pl.ds(here ^ (4 * q + m), 1), :] = line[:, m * BLK : (m + 1) * BLK]


STEP = 256


def gram_kernel(which, rows, rhs, col_sq, tot, last, setup=None):
    slots = 4
    held = pieces_of(which)
    away = {PIECES[p][0]: p for p in held if not PIECES[p][3]}
    steps = range(0, COLS, STEP)
    order = in_turn([(q, at) for q in which if q in away for at in steps], [(q, at) for q in which if q not in away for at in steps])
    most = max([PIECES[p][2] for p in away.values()] or [8])
    count = len(which)
    first = setup is not None

    def body(*refs):
        rows_of = dict(zip(which, refs[:count]))
        given, refs = refs[count : count + 3], refs[count + 3 :]
        if first:
            near_ref, far_ref, _ = given
            rhs, col_sq, tot_ref, refs = refs[0], refs[1], refs[2], refs[3:]
        else:
            rhs, col_sq, _ = given
            tot_ref, refs = refs[0], refs[1:]
        if last:
            out_ref, refs = refs[0], refs[1:]
        tile_of, refs = dict(zip(held, refs[: len(held)])), refs[len(held) :]
        own = {q: refs[3 * n : 3 * n + 3] for n, q in enumerate(which)}
        stage, sems = refs[3 * count :]
        sent = []

        def send(n):
            q, at = sent[n]
            rows = PIECES[away[q]][2]
            return pltpu.make_async_copy(
                stage.at[n % slots, pl.ds(0, rows), :], tile_of[away[q]].at[:, pl.ds(at, STEP)], sems.at[n % slots]
            )

        if first:
            col_setup(near_ref, far_ref, rhs, col_sq)
        waited = 0
        for q, at in order:
            lhs, row_sq, acc = own[q]
            if at == 0:
                row_setup(rows_of[q], lhs, row_sq)
            n = len(sent)
            if q in away and n >= slots:
                send(n - slots).wait()
                waited = n - slots + 1
            outs = []
            for p in pieces_of((q,)):
                _, start, rows, kept = PIECES[p]
                outs.append((tile_of[p], start, rows, at) if kept else (stage.at[n % slots], start, rows, 0))
            sums = gram_part(lhs, rhs, row_sq, col_sq, at, outs)
            acc[...] = sums if at == 0 else acc[...] + sums
            if q in away:
                sent.append((q, at))
                send(n).start()
        for q in which:
            put_totals(own[q][2][...], tot_ref, q)
        if last:
            for n in range(16):
                out_ref[n] = tot_ref[...]
        for n in range(waited, len(sent)):
            send(n).wait()

    if first:
        given = [*setup, tot]
        made = [jax.ShapeDtypeStruct((COLS, 256), bf16), dense(1, COLS)]
    else:
        given, made = [rhs, col_sq, tot], []
    here = len(made)
    scratch = [pltpu.VMEM((QUART, 256), bf16), pltpu.VMEM((QUART, 128), f32), pltpu.VMEM((QUART, 128), f32)] * count
    scratch += [pltpu.VMEM((slots, most, STEP), f32), pltpu.SemaphoreType.DMA((slots,))]
    out = made + [dense(16, BLK)] + ([dense(16, 16, BLK)] if last else [])
    return pl.pallas_call(
        body,
        in_specs=[WHOLE] * (count + 3),
        out_specs=[WHOLE] * len(out) + [tile_spec(p) for p in held],
        out_shape=out + [tile_shape(p) for p in held],
        input_output_aliases={count + 2: here},
        scratch_shapes=scratch,
        compiler_params=params(12 if last else 16),
        name="gram",
    )(*rows, *given)


SLOTS = 4


def apply_down(rows, totals, tiles):
    every = range(4)
    count = len(PIECES)
    far = units_of(every, False)
    order = in_turn(units_of(every, True), far)

    def body(*refs):
        row_refs, parts_ref, tile_refs = refs[0:4], refs[4], refs[5 : 5 + count]
        other_ref, own_ref, own_tot = refs[5 + count : 8 + count]
        weights, out, tot_ref, held, sems = refs[8 + 2 * count :]

        def fetch(n):
            p, at = far[n]
            return pltpu.make_async_copy(
                tile_refs[p].at[pl.ds(at, UNIT), :], held.at[n % SLOTS], sems.at[n % SLOTS]
            )

        for n in range(SLOTS):
            fetch(n).start()
        here = place()
        total = parts_ref[0]
        for n in range(1, 16):
            total = total + parts_ref[n]
        tot_ref[...] = total
        own_tot[...] = jnp.broadcast_to(tot_ref[pl.ds(here, 1), :], (8, BLK))
        for q in range(4):
            blocks = [
                values_of(row_refs[q], b * LINES + PTS) / tot_ref[pl.ds(here ^ (4 * q + b), 1), :]
                for b in range(4)
            ]
            high, low = two_terms(jnp.concatenate(blocks, axis=1))
            weights[:, q * QUART : (q + 1) * QUART] = jnp.concatenate([high, low], axis=0)
        first, n = True, 0
        for p, at in order:
            kept = PIECES[p][3]
            if kept:
                piece = tile_refs[p][at : at + UNIT, :]
            else:
                fetch(n).wait()
                piece = held[n % SLOTS]
            start = PIECES[p][0] * QUART + PIECES[p][1] + at
            w = weights[:, start : start + UNIT]
            hi, lo = two_terms(piece)
            part = jnp.dot(w, hi, preferred_element_type=f32) + jnp.dot(w, lo, preferred_element_type=f32)
            part = part[0:16] + part[16:32]
            if first:
                out[...] = part
                first = False
            else:
                out[...] += part
            if not kept:
                if n + SLOTS < len(far):
                    fetch(n + SLOTS).start()
                n += 1
        own_ref[...] = out[:, 0:HALF]
        other_ref[...] = out[:, HALF:COLS]

    return pl.pallas_call(
        body,
        in_specs=[WHOLE] * 5 + [tile_spec(p) for p in range(count)],
        out_specs=[WHOLE] * 3 + [tile_spec(p) for p in range(count)],
        out_shape=[dense(TGT, HALF)] * 2 + [dense(8, BLK)] + [tile_shape(p) for p in range(count)],
        input_output_aliases={5 + p: 3 + p for p in range(count)},
        scratch_shapes=[
            pltpu.VMEM((32, 4 * QUART), bf16),
            pltpu.VMEM((TGT, COLS), f32),
            pltpu.VMEM((16, BLK), f32),
            pltpu.VMEM((SLOTS, UNIT, COLS), f32),
            pltpu.SemaphoreType.DMA((SLOTS,)),
        ],
        compiler_params=params(13),
        name="apply_down",
    )(*rows, totals, *tiles)


def pack(own, got, totals):
    def body(own_ref, got_ref, tot_ref, out_ref):
        out_ref[:, 0:QUART] = own_ref[...] + got_ref[...]
        out_ref[:, QUART : QUART + 128] = jnp.zeros((TGT, 128), f32)
        out_ref[0:1, QUART : QUART + 128] = tot_ref[0:1, 0:128]
        out_ref[1:2, QUART : QUART + 128] = tot_ref[0:1, 128:256]
        out_ref[2:3, QUART : QUART + 64] = tot_ref[0:1, 256:320]

    return pl.pallas_call(
        body,
        in_specs=[WHOLE] * 3,
        out_specs=WHOLE,
        out_shape=dense(TGT, QUART + 128),
        compiler_params=params(),
        name="pack",
    )(own, got, totals)


def first_update(packed, ahead):
    def body(a0, a1, a2, a3, ahead_ref, weighted_ref, scaled_ref):
        refs = (a0, a1, a2, a3)
        scaled = []
        for m in range(4):
            applied = None
            for j in range(4):
                at = (m ^ j) * BLK
                term = refs[j][:, at : at + BLK]
                applied = term if applied is None else applied + term
            weighted = values_of(ahead_ref, m * VALS) - applied
            if m == 0:
                weighted_ref[...] = weighted
            line = refs[m][0:8, QUART : QUART + 128]
            line = jnp.concatenate([line[0:1, :], line[1:2, :], line[2:3, 0:64]], axis=1)
            scaled.append(weighted / line)
        scaled_ref[...] = jnp.concatenate(scaled, axis=1)

    return pl.pallas_call(
        body,
        in_specs=[WHOLE] * 5,
        out_specs=[WHOLE] * 2,
        out_shape=[dense(TGT, BLK), dense(TGT, QUART)],
        compiler_params=params(),
        name="first_update",
    )(*packed, ahead)


def apply_across(own, other, tiles, which):
    pieces = pieces_of(which)
    kept, far = units_of(which, True), units_of(which, False)
    lead = max(len(kept) - len(far), 0)
    order = kept[:lead] + in_turn(kept[lead:], far)
    slots = 4
    count = len(which)

    def body(*refs):
        own_ref, other_ref = refs[0:2]
        refs = refs[2:]
        tile_refs, refs = dict(zip(pieces, refs[: len(pieces)])), refs[len(pieces) :]
        out_refs, refs = dict(zip(which, refs[:count])), refs[count:]
        weights, held, sems = refs[len(pieces) :]

        def fetch(n):
            p, at = far[n]
            return pltpu.make_async_copy(
                tile_refs[p].at[pl.ds(at, UNIT), :], held.at[n % slots], sems.at[n % slots]
            )

        for n in range(min(slots, len(far))):
            fetch(n).start()
        for half, ref in ((0, own_ref), (1, other_ref)):
            high, low = two_terms(ref[...].T)
            weights[half * HALF : (half + 1) * HALF, :] = jnp.concatenate([high, low], axis=1)
        n = 0
        for p, at in order:
            q, start, _, stays = PIECES[p]
            if stays:
                piece = tile_refs[p][at : at + UNIT, :]
            else:
                fetch(n).wait()
                piece = held[n % slots]
            hi, lo = two_terms(piece)
            w = weights[...]
            part = jnp.dot(hi, w, preferred_element_type=f32) + jnp.dot(lo, w, preferred_element_type=f32)
            part = part.T
            out_refs[q][:, start + at : start + at + UNIT] = part[0:16] + part[16:32]
            if not stays:
                if n + slots < len(far):
                    fetch(n + slots).start()
                n += 1

    return pl.pallas_call(
        body,
        in_specs=[WHOLE] * 2 + [tile_spec(p) for p in pieces],
        out_specs=[WHOLE] * count + [tile_spec(p) for p in pieces],
        out_shape=[dense(TGT, QUART)] * count + [tile_shape(p) for p in pieces],
        input_output_aliases={2 + n: count + n for n in range(len(pieces))},
        scratch_shapes=[
            pltpu.VMEM((COLS, 32), bf16),
            pltpu.VMEM((slots, UNIT, COLS), f32),
            pltpu.SemaphoreType.DMA((slots,)),
        ],
        compiler_params=params(14),
        name="apply_across",
    )(own, other, *[tiles[p] for p in pieces])[:count]


def add_blocks(arrays):
    def body(a0, a1, a2, a3, o0, o1, o2, o3):
        total = (a0[...] + a1[...]) + (a2[...] + a3[...])
        for m, ref in enumerate((o0, o1, o2, o3)):
            ref[...] = total[:, m * BLK : (m + 1) * BLK]

    return pl.pallas_call(
        body,
        in_specs=[WHOLE] * 4,
        out_specs=[WHOLE] * 4,
        out_shape=[dense(TGT, BLK)] * 4,
        compiler_params=params(),
        name="add_blocks",
    )(*arrays)


def last_update(applied, weighted, goal):
    def body(a0, a1, a2, a3, weighted_ref, goal_ref, out_ref, residual_ref):
        applied = (a0[...] + a1[...]) + (a2[...] + a3[...])
        weighted = weighted_ref[...]
        residual = goal_ref[...] - applied - ridge_term * weighted
        residual_ref[...] = residual
        out_ref[...] = weighted + residual

    return pl.pallas_call(
        body,
        in_specs=[WHOLE] * 6,
        out_specs=[WHOLE] * 2,
        out_shape=[dense(TGT, BLK)] * 2,
        compiler_params=params(),
        name="last_update",
    )(*applied, weighted, goal)


def swap(x, axis, by):
    n = 2 if axis == "k" else 4
    return lax.ppermute(x, axis, [(i, i ^ by) for i in range(n)])


def spread(x, axis):
    return [x] + [swap(x, axis, m) for m in (1, 2, 3)]


def per_device(centres, targets, start_weights):
    pts, goal, start = centres.T, targets.T, start_weights.T
    row_block, col_block = pack_blocks(pts, goal, start)
    row_pair = join_pair(row_block, swap(row_block, "z", 1))
    col_pair = join_pair(col_block, swap(col_block, "y", 1))
    row_own = join_rows(row_pair, swap(row_pair, "z", 3))
    near, ahead = join_cols(col_pair, swap(col_pair, "y", 3))
    far = swap(near, "k", 1)
    rows = spread(row_own, X)

    tot = jnp.zeros((16, BLK), f32)
    tiles = [None] * len(PIECES)
    rhs, col_sq, tot, *tiles[0:2] = gram_kernel((0,), rows[:1], None, None, tot, False, (near, far))
    tot, *tiles[3:5] = gram_kernel((2, 3), rows[2:], rhs, col_sq, tot, False)
    tot, parts, tiles[2] = gram_kernel((1,), rows[1:2], rhs, col_sq, tot, True)
    parts = lax.all_to_all(parts, ("xl", "xh", "z"), 0, 0)

    other, own, tot, *tiles = apply_down(rows, parts, tiles)
    packed = spread(pack(own, swap(other, "k", 1), tot), "y")
    weighted, scaled = first_update(packed, ahead)

    scaled_other = swap(scaled, "k", 1)
    parts = apply_across(scaled, scaled_other, tiles, (1, 2, 3))
    parts = [swap(part, X, q) for q, part in zip((1, 2, 3), parts)]
    parts += apply_across(scaled, scaled_other, tiles, (0,))
    blocks = add_blocks(parts)
    blocks = [blocks[0]] + [swap(blocks[m], "z", m) for m in (1, 2, 3)]
    weighted, residual = last_update(blocks, weighted, goal)
    return weighted.T, residual.T


def solution(mesh):
    fine = Mesh(mesh.devices.reshape(4, 2, 2, 4, 2), AXES)
    placed = P(AXES, None)
    return jax.shard_map(
        per_device, mesh=fine, in_specs=(placed,) * 3, out_specs=(placed,) * 2, check_vma=False
    )
```

```python
import jax
import jax.numpy as jnp
from jax import lax
from jax.experimental import pallas as pl
from jax.experimental.pallas import tpu as pltpu
from jax.sharding import Mesh, PartitionSpec as P

ITERS = 2

kernel_width = 2.0
soften = 0.01
ridge_term = 0.25

SCALE = 1.4426950408889634 / kernel_width
FLOOR = soften * SCALE * SCALE

f32 = jnp.float32
bf16 = jnp.bfloat16

AXES = ("y", "xl", "xh", "z", "k")
X = ("xl", "xh")
BLK = 320
FEAT = 64
TGT = 16
QUART = 4 * BLK
COLS = 8 * BLK
HALF = COLS // 2
PIECES = (
    (0, 0, 256, True),
    (0, 256, 1024, False),
    (1, 0, 1280, True),
    (2, 0, 1280, True),
    (3, 0, 1280, False),
)
UNIT = 256


def pieces_of(which):
    return [p for p, piece in enumerate(PIECES) if piece[0] in which]


def units_of(which, kept):
    return [(p, at) for p in pieces_of(which) if PIECES[p][3] == kept for at in range(0, PIECES[p][2], UNIT)]


def in_turn(lead, rest):
    order = []
    for n in range(max(len(lead), len(rest))):
        order += lead[n : n + 1] + rest[n : n + 1]
    return order

WHOLE = pl.BlockSpec(memory_space=pltpu.VMEM)
FAR = pl.BlockSpec(memory_space=pltpu.HBM)

NT = (((1,), (1,)), ((), ()))


def params(mib=12):
    return pltpu.CompilerParams(vmem_limit_bytes=mib << 20)


def tile_spec(p):
    return WHOLE if PIECES[p][3] else FAR


def tile_shape(p):
    return (pltpu.VMEM if PIECES[p][3] else pltpu.HBM)((PIECES[p][2], COLS), f32)


def dense(*shape):
    return jax.ShapeDtypeStruct(shape, f32)


def two_terms(vals):
    high = vals.astype(bf16)
    return high, (vals - high.astype(f32)).astype(bf16)


LINES = 200
PTS = 160
VALS = LINES - PTS


def pack_values(out_ref, vals):
    out_ref[160:176, :] = vals[:, 0:128]
    out_ref[176:192, :] = vals[:, 128:256]
    out_ref[192:200, :] = jnp.concatenate([vals[0:8, 256:320], vals[8:16, 256:320]], axis=1)


def values_of(ref, at):
    tail = ref[at + 32 : at + 40, :]
    tail = jnp.concatenate([tail[:, 0:64], tail[:, 64:128]], axis=0)
    return jnp.concatenate([ref[at : at + 16, :], ref[at + 16 : at + 32, :], tail], axis=1)


def pack_blocks(pts, goal, start):
    def body(pts_far, goal_far, start_far, row_ref, col_ref, pts_ref, goal_ref, start_ref, sems):
        copies = [
            pltpu.make_async_copy(src, dst, sems.at[n])
            for n, (src, dst) in enumerate(((pts_far, pts_ref), (goal_far, goal_ref), (start_far, start_ref)))
        ]
        for copy in copies:
            copy.start()
        for copy in copies:
            copy.wait()
        flat = pts_ref[...].T
        both = jnp.concatenate([flat[0:PTS, :], flat[PTS:BLK, :]], axis=1)
        row_ref[0:PTS, :] = both
        col_ref[0:PTS, :] = both
        start = start_ref[...]
        pack_values(row_ref, start)
        pack_values(col_ref, goal_ref[...] + (1.0 - ridge_term) * start)

    return pl.pallas_call(
        body,
        in_specs=[pl.BlockSpec(memory_space=pl.ANY)] * 3,
        out_specs=[WHOLE] * 2,
        out_shape=[dense(LINES, 128)] * 2,
        scratch_shapes=[
            pltpu.VMEM((FEAT, BLK), f32),
            pltpu.VMEM((TGT, BLK), f32),
            pltpu.VMEM((TGT, BLK), f32),
            pltpu.SemaphoreType.DMA((3,)),
        ],
        compiler_params=params(),
        name="pack_blocks",
    )(pts, goal, start)


def join_pair(own, got):
    def body(own_ref, got_ref, out_ref):
        out_ref[0:LINES, :] = own_ref[...]
        out_ref[LINES : 2 * LINES, :] = got_ref[...]

    return pl.pallas_call(
        body,
        in_specs=[WHOLE] * 2,
        out_specs=WHOLE,
        out_shape=dense(2 * LINES, 128),
        compiler_params=params(),
        name="join_pair",
    )(own, got)


PAIRS = ((0, 0), (0, 1), (1, 1), (1, 0))


def join_rows(own, got):
    def body(own_ref, got_ref, out_ref):
        for m, (pair, at) in enumerate(PAIRS):
            ref = (own_ref, got_ref)[pair]
            out_ref[m * LINES : (m + 1) * LINES, :] = ref[at * LINES : (at + 1) * LINES, :]

    return pl.pallas_call(
        body,
        in_specs=[WHOLE] * 2,
        out_specs=WHOLE,
        out_shape=dense(4 * LINES, 128),
        compiler_params=params(),
        name="join_rows",
    )(own, got)


def join_cols(own, got):
    def body(own_ref, got_ref, near_ref, ahead_ref):
        for m, (pair, at) in enumerate(PAIRS):
            ref, at = (own_ref, got_ref)[pair], at * LINES
            near_ref[m * PTS : (m + 1) * PTS, :] = ref[at : at + PTS, :]
            ahead_ref[m * VALS : (m + 1) * VALS, :] = ref[at + PTS : at + LINES, :]

    return pl.pallas_call(
        body,
        in_specs=[WHOLE] * 2,
        out_specs=[WHOLE] * 2,
        out_shape=[dense(4 * PTS, 128), dense(4 * VALS, 128)],
        compiler_params=params(),
        name="join_cols",
    )(own, got)


def point_terms(lines):
    high, low = two_terms(lines * SCALE)
    kept = high.astype(f32) + low.astype(f32)
    return high, low, kept * kept


def row_setup(rows_ref, lhs, row_sq):
    for b in range(4):
        high, low, sq = point_terms(rows_ref[b * LINES : b * LINES + PTS, :])
        for half in range(2):
            at = b * BLK + half * PTS
            side = slice(64 * half, 64 * half + 64)
            hi, lo = high[:, side], low[:, side]
            lhs[at : at + PTS, :] = jnp.concatenate([hi, hi, lo, lo], axis=1) * jnp.asarray(2.0, bf16)
            total = jnp.sum(sq[:, side], axis=1, keepdims=True) + FLOOR
            row_sq[at : at + PTS, :] = jnp.broadcast_to(total, (PTS, 128))


def col_setup(near_ref, far_ref, rhs, col_sq):
    lines = []
    for core, ref in enumerate((near_ref, far_ref)):
        for m in range(4):
            high, low, sq = point_terms(ref[m * PTS : (m + 1) * PTS, :])
            flat = sq.T
            for half in range(2):
                at = (core * 4 + m) * BLK + half * PTS
                side = slice(64 * half, 64 * half + 64)
                hi, lo = high[:, side], low[:, side]
                rhs[at : at + PTS, :] = jnp.concatenate([hi, lo, hi, lo], axis=1)
                lines.append(jnp.sum(flat[side, :], axis=0, keepdims=True))
    col_sq[...] = jnp.concatenate(lines, axis=1)


def gram_part(lhs, rhs, row_sq, col_sq, at, outs):
    cross = lax.dot_general(lhs[...], rhs[at : at + STEP, :], NT, preferred_element_type=f32)
    sums = None
    for lane in range(0, STEP, 128):
        minus = (cross[:, lane : lane + 128] - row_sq[...]) - col_sq[:, at + lane : at + lane + 128]
        part = jnp.exp2(minus * lax.rsqrt(jnp.abs(minus)))
        for out, start, rows, to in outs:
            out[0:rows, to + lane : to + lane + 128] = part[start : start + rows, :]
        sums = part if sums is None else sums + part
    return sums


def place():
    return (lax.axis_index("xl") * 2 + lax.axis_index("xh")) * 4 + lax.axis_index("z")


def put_totals(acc, tot_ref, q):
    line = jnp.sum(acc.T, axis=0, keepdims=True)
    here = place()
    for m in range(4):
        tot_ref[pl.ds(here ^ (4 * q + m), 1), :] = line[:, m * BLK : (m + 1) * BLK]


STEP = 256


def gram_kernel(which, rows, rhs, col_sq, tot, last, setup=None):
    slots = 4
    held = pieces_of(which)
    away = {PIECES[p][0]: p for p in held if not PIECES[p][3]}
    steps = range(0, COLS, STEP)
    order = in_turn([(q, at) for q in which if q in away for at in steps], [(q, at) for q in which if q not in away for at in steps])
    most = max([PIECES[p][2] for p in away.values()] or [8])
    count = len(which)
    first = setup is not None

    def body(*refs):
        rows_of = dict(zip(which, refs[:count]))
        given, refs = refs[count : count + 3], refs[count + 3 :]
        if first:
            near_ref, far_ref, _ = given
            rhs, col_sq, tot_ref, refs = refs[0], refs[1], refs[2], refs[3:]
        else:
            rhs, col_sq, _ = given
            tot_ref, refs = refs[0], refs[1:]
        if last:
            out_ref, refs = refs[0], refs[1:]
        tile_of, refs = dict(zip(held, refs[: len(held)])), refs[len(held) :]
        own = {q: refs[3 * n : 3 * n + 3] for n, q in enumerate(which)}
        stage, sems = refs[3 * count :]
        sent = []

        def send(n):
            q, at = sent[n]
            rows = PIECES[away[q]][2]
            return pltpu.make_async_copy(
                stage.at[n % slots, pl.ds(0, rows), :], tile_of[away[q]].at[:, pl.ds(at, STEP)], sems.at[n % slots]
            )

        if first:
            col_setup(near_ref, far_ref, rhs, col_sq)
        waited = 0
        for q, at in order:
            lhs, row_sq, acc = own[q]
            if at == 0:
                row_setup(rows_of[q], lhs, row_sq)
            n = len(sent)
            if q in away and n >= slots:
                send(n - slots).wait()
                waited = n - slots + 1
            outs = []
            for p in pieces_of((q,)):
                _, start, rows, kept = PIECES[p]
                outs.append((tile_of[p], start, rows, at) if kept else (stage.at[n % slots], start, rows, 0))
            sums = gram_part(lhs, rhs, row_sq, col_sq, at, outs)
            acc[...] = sums if at == 0 else acc[...] + sums
            if q in away:
                sent.append((q, at))
                send(n).start()
        for q in which:
            put_totals(own[q][2][...], tot_ref, q)
        if last:
            for n in range(16):
                out_ref[n] = tot_ref[...]
        for n in range(waited, len(sent)):
            send(n).wait()

    if first:
        given = [*setup, tot]
        made = [jax.ShapeDtypeStruct((COLS, 256), bf16), dense(1, COLS)]
    else:
        given, made = [rhs, col_sq, tot], []
    here = len(made)
    scratch = [pltpu.VMEM((QUART, 256), bf16), pltpu.VMEM((QUART, 128), f32), pltpu.VMEM((QUART, 128), f32)] * count
    scratch += [pltpu.VMEM((slots, most, STEP), f32), pltpu.SemaphoreType.DMA((slots,))]
    out = made + [dense(16, BLK)] + ([dense(16, 16, BLK)] if last else [])
    return pl.pallas_call(
        body,
        in_specs=[WHOLE] * (count + 3),
        out_specs=[WHOLE] * len(out) + [tile_spec(p) for p in held],
        out_shape=out + [tile_shape(p) for p in held],
        input_output_aliases={count + 2: here},
        scratch_shapes=scratch,
        compiler_params=params(12 if last else 16),
        name="gram",
    )(*rows, *given)


SLOTS = 4


def apply_down(rows, totals, tiles):
    every = range(4)
    count = len(PIECES)
    far = units_of(every, False)
    order = in_turn(units_of(every, True), far)

    def body(*refs):
        row_refs, parts_ref, tile_refs = refs[0:4], refs[4], refs[5 : 5 + count]
        other_ref, own_ref, own_tot = refs[5 + count : 8 + count]
        weights, out, tot_ref, held, sems = refs[8 + 2 * count :]

        def fetch(n):
            p, at = far[n]
            return pltpu.make_async_copy(
                tile_refs[p].at[pl.ds(at, UNIT), :], held.at[n % SLOTS], sems.at[n % SLOTS]
            )

        for n in range(SLOTS):
            fetch(n).start()
        here = place()
        total = parts_ref[0]
        for n in range(1, 16):
            total = total + parts_ref[n]
        tot_ref[...] = total
        own_tot[...] = jnp.broadcast_to(tot_ref[pl.ds(here, 1), :], (8, BLK))
        for q in range(4):
            blocks = [
                values_of(row_refs[q], b * LINES + PTS) / tot_ref[pl.ds(here ^ (4 * q + b), 1), :]
                for b in range(4)
            ]
            high, low = two_terms(jnp.concatenate(blocks, axis=1))
            weights[:, q * QUART : (q + 1) * QUART] = jnp.concatenate([high, low], axis=0)
        first, n = True, 0
        for p, at in order:
            kept = PIECES[p][3]
            if kept:
                piece = tile_refs[p][at : at + UNIT, :]
            else:
                fetch(n).wait()
                piece = held[n % SLOTS]
            start = PIECES[p][0] * QUART + PIECES[p][1] + at
            w = weights[:, start : start + UNIT]
            hi, lo = two_terms(piece)
            part = jnp.dot(w, hi, preferred_element_type=f32) + jnp.dot(w, lo, preferred_element_type=f32)
            part = part[0:16] + part[16:32]
            if first:
                out[...] = part
                first = False
            else:
                out[...] += part
            if not kept:
                if n + SLOTS < len(far):
                    fetch(n + SLOTS).start()
                n += 1
        own_ref[...] = out[:, 0:HALF]
        other_ref[...] = out[:, HALF:COLS]

    return pl.pallas_call(
        body,
        in_specs=[WHOLE] * 5 + [tile_spec(p) for p in range(count)],
        out_specs=[WHOLE] * 3 + [tile_spec(p) for p in range(count)],
        out_shape=[dense(TGT, HALF)] * 2 + [dense(8, BLK)] + [tile_shape(p) for p in range(count)],
        input_output_aliases={5 + p: 3 + p for p in range(count)},
        scratch_shapes=[
            pltpu.VMEM((32, 4 * QUART), bf16),
            pltpu.VMEM((TGT, COLS), f32),
            pltpu.VMEM((16, BLK), f32),
            pltpu.VMEM((SLOTS, UNIT, COLS), f32),
            pltpu.SemaphoreType.DMA((SLOTS,)),
        ],
        compiler_params=params(13),
        name="apply_down",
    )(*rows, totals, *tiles)


def pack(own, got, totals):
    def body(own_ref, got_ref, tot_ref, out_ref):
        out_ref[:, 0:QUART] = own_ref[...] + got_ref[...]
        out_ref[:, QUART : QUART + 128] = jnp.zeros((TGT, 128), f32)
        out_ref[0:1, QUART : QUART + 128] = tot_ref[0:1, 0:128]
        out_ref[1:2, QUART : QUART + 128] = tot_ref[0:1, 128:256]
        out_ref[2:3, QUART : QUART + 64] = tot_ref[0:1, 256:320]

    return pl.pallas_call(
        body,
        in_specs=[WHOLE] * 3,
        out_specs=WHOLE,
        out_shape=dense(TGT, QUART + 128),
        compiler_params=params(),
        name="pack",
    )(own, got, totals)


def first_update(packed, ahead):
    def body(a0, a1, a2, a3, ahead_ref, weighted_ref, scaled_ref):
        refs = (a0, a1, a2, a3)
        scaled = []
        for m in range(4):
            applied = None
            for j in range(4):
                at = (m ^ j) * BLK
                term = refs[j][:, at : at + BLK]
                applied = term if applied is None else applied + term
            weighted = values_of(ahead_ref, m * VALS) - applied
            if m == 0:
                weighted_ref[...] = weighted
            line = refs[m][0:8, QUART : QUART + 128]
            line = jnp.concatenate([line[0:1, :], line[1:2, :], line[2:3, 0:64]], axis=1)
            scaled.append(weighted / line)
        scaled_ref[...] = jnp.concatenate(scaled, axis=1)

    return pl.pallas_call(
        body,
        in_specs=[WHOLE] * 5,
        out_specs=[WHOLE] * 2,
        out_shape=[dense(TGT, BLK), dense(TGT, QUART)],
        compiler_params=params(),
        name="first_update",
    )(*packed, ahead)


def apply_across(own, other, tiles, which):
    pieces = pieces_of(which)
    kept, far = units_of(which, True), units_of(which, False)
    lead = max(len(kept) - len(far), 0)
    order = kept[:lead] + in_turn(kept[lead:], far)
    slots, depth = 4, 2
    count = len(which)

    def body(*refs):
        own_ref, other_ref = refs[0:2]
        refs = refs[2:]
        tile_refs, refs = dict(zip(pieces, refs[: len(pieces)])), refs[len(pieces) :]
        out_refs, refs = dict(zip(which, refs[:count])), refs[count:]
        weights, held, sems = refs[len(pieces) :]

        def fetch(n):
            p, at = far[n]
            return pltpu.make_async_copy(
                tile_refs[p].at[pl.ds(at, UNIT), :], held.at[n % slots], sems.at[n % slots]
            )

        for n in range(min(depth, len(far))):
            fetch(n).start()
        for half, ref in ((0, own_ref), (1, other_ref)):
            high, low = two_terms(ref[...].T)
            weights[half * HALF : (half + 1) * HALF, :] = jnp.concatenate([high, low], axis=1)
        n = 0
        for p, at in order:
            q, start, _, stays = PIECES[p]
            if stays:
                piece = tile_refs[p][at : at + UNIT, :]
            else:
                fetch(n).wait()
                if n + depth < len(far):
                    fetch(n + depth).start()
                piece = held[n % slots]
            hi, lo = two_terms(piece)
            w = weights[...]
            part = jnp.dot(hi, w, preferred_element_type=f32) + jnp.dot(lo, w, preferred_element_type=f32)
            part = part.T
            out_refs[q][:, start + at : start + at + UNIT] = part[0:16] + part[16:32]
            if not stays:
                n += 1

    return pl.pallas_call(
        body,
        in_specs=[WHOLE] * 2 + [tile_spec(p) for p in pieces],
        out_specs=[WHOLE] * count + [tile_spec(p) for p in pieces],
        out_shape=[dense(TGT, QUART)] * count + [tile_shape(p) for p in pieces],
        input_output_aliases={2 + n: count + n for n in range(len(pieces))},
        scratch_shapes=[
            pltpu.VMEM((COLS, 32), bf16),
            pltpu.VMEM((slots, UNIT, COLS), f32),
            pltpu.SemaphoreType.DMA((slots,)),
        ],
        compiler_params=params(14),
        name="apply_across",
    )(own, other, *[tiles[p] for p in pieces])[:count]


def add_blocks(arrays):
    def body(a0, a1, a2, a3, o0, o1, o2, o3):
        total = (a0[...] + a1[...]) + (a2[...] + a3[...])
        for m, ref in enumerate((o0, o1, o2, o3)):
            ref[...] = total[:, m * BLK : (m + 1) * BLK]

    return pl.pallas_call(
        body,
        in_specs=[WHOLE] * 4,
        out_specs=[WHOLE] * 4,
        out_shape=[dense(TGT, BLK)] * 4,
        compiler_params=params(),
        name="add_blocks",
    )(*arrays)


def last_update(applied, weighted, goal):
    def body(a0, a1, a2, a3, weighted_ref, goal_ref, out_ref, residual_ref):
        applied = (a0[...] + a1[...]) + (a2[...] + a3[...])
        weighted = weighted_ref[...]
        residual = goal_ref[...] - applied - ridge_term * weighted
        residual_ref[...] = residual
        out_ref[...] = weighted + residual

    return pl.pallas_call(
        body,
        in_specs=[WHOLE] * 6,
        out_specs=[WHOLE] * 2,
        out_shape=[dense(TGT, BLK)] * 2,
        compiler_params=params(),
        name="last_update",
    )(*applied, weighted, goal)


def swap(x, axis, by):
    n = 2 if axis == "k" else 4
    return lax.ppermute(x, axis, [(i, i ^ by) for i in range(n)])


def spread(x, axis):
    return [x] + [swap(x, axis, m) for m in (1, 2, 3)]


def per_device(centres, targets, start_weights):
    pts, goal, start = centres.T, targets.T, start_weights.T
    row_block, col_block = pack_blocks(pts, goal, start)
    row_pair = join_pair(row_block, swap(row_block, "z", 1))
    col_pair = join_pair(col_block, swap(col_block, "y", 1))
    row_own = join_rows(row_pair, swap(row_pair, "z", 3))
    near, ahead = join_cols(col_pair, swap(col_pair, "y", 3))
    far = swap(near, "k", 1)
    rows = spread(row_own, X)

    tot = jnp.zeros((16, BLK), f32)
    tiles = [None] * len(PIECES)
    rhs, col_sq, tot, *tiles[0:2] = gram_kernel((0,), rows[:1], None, None, tot, False, (near, far))
    tot, *tiles[3:5] = gram_kernel((2, 3), rows[2:], rhs, col_sq, tot, False)
    tot, parts, tiles[2] = gram_kernel((1,), rows[1:2], rhs, col_sq, tot, True)
    parts = lax.all_to_all(parts, ("xl", "xh", "z"), 0, 0)

    other, own, tot, *tiles = apply_down(rows, parts, tiles)
    packed = spread(pack(own, swap(other, "k", 1), tot), "y")
    weighted, scaled = first_update(packed, ahead)

    scaled_other = swap(scaled, "k", 1)
    parts = apply_across(scaled, scaled_other, tiles, (1, 2, 3))
    parts = [swap(part, X, q) for q, part in zip((1, 2, 3), parts)]
    parts += apply_across(scaled, scaled_other, tiles, (0,))
    blocks = add_blocks(parts)
    blocks = [blocks[0]] + [swap(blocks[m], "z", m) for m in (1, 2, 3)]
    weighted, residual = last_update(blocks, weighted, goal)
    return weighted.T, residual.T


def solution(mesh):
    fine = Mesh(mesh.devices.reshape(4, 2, 2, 4, 2), AXES)
    placed = P(AXES, None)
    return jax.shard_map(
        per_device, mesh=fine, in_specs=(placed,) * 3, out_specs=(placed,) * 2, check_vma=False
    )
```
